32 devices in a mesh: slab: 4 (over x, core), src: 8 (over z, y).
Axes of the slice: x: 2, y: 2, z: 4, core: 2. Of those that a mesh axis runs over, the one named last changes fastest.
Arguments:
- trace_values: bfloat16 [8, 2048, 512], P('src', 'slab'), may hold values from -6 to 6
- trace_owner: int32 [8, 2048, 1], P('src', 'slab'), may hold values from 0 to 3; in each aligned block of 512 rows (0 to 511, 512 to 1023, ..., all dimensions but the last counted through in order) at most 256 rows name the same one
- trace_source: int32 [8, 2048], P('src', 'slab'), may hold values from 0 to 511
- source_fields: bfloat16 [2, 2048, 4096], P(None, 'slab', 'src'), may hold values from -0.0625 to 0.0625
- green_fields: bfloat16 [2, 2048, 4096], P(None, 'slab', 'src'), may hold values from -0.0625 to 0.0625
Outputs:
- gradient: float32 [4096], P('src')
The draws below stay inside these ranges and needn't reach their ends.
Inputs may be any that keep to these rules, and one draw needn't show every extreme that they name: `trace_owner`: among the traces of one device, no owner is named by more than 256 traces, a bound that some block reaches.
All inputs are finite; a program needn't handle non-finite values.
Results may differ from the reference program's by a relative error of at most 0.0026.
Values may be sent and summed in bfloat16 or wider, within the bound.
No kernel may reach another device: no remote copies, remote signals or barrier semaphores. Data moves between devices by JAX's collectives and lax.ppermute only.
A program may use at most 64 MiB of HBM per device.

```python
import math
import jax
import jax.numpy as jnp
import numpy as np
from jax import lax

NREC = 2048
S_DEV = 512
M_DEV = 512
TR_DEV = 512
CAP = 256
NSRC = 2048
M = 4096
RB = 256
TRACES = 2048
N_SLAB = 4
N_SRC = 8


def set_ends(values, rng, low, largest):
    longest = values.shape.index(max(values.shape))
    spots = []
    for shift in (0, 1):
        where = [jax.random.randint(jax.random.fold_in(rng, axis), (), 0, length) for axis, length in enumerate(values.shape)]
        where[longest] = (where[longest] + shift) % values.shape[longest]
        spots.append(tuple(where))
    return values.at[spots[0]].set(low).at[spots[1]].set(largest)


def block_scale(stream_key, extent, pieces, low, largest):
    factor_of = 1.0
    for position, blocks in pieces:
        steps = jax.random.uniform(jax.random.fold_in(jax.random.fold_in(stream_key, 6), position), (blocks,), jnp.float32, low / len(pieces), largest / len(pieces))
        factor_of = factor_of * jnp.repeat(jnp.exp(steps), extent[position] // blocks).reshape((-1,) + (1,) * (len(extent) - 1 - position))
    return factor_of


def assign_block(key, own, number, rows, amount, top, most, skew):
    sequence = jax.random.permutation(key, amount)
    packed, usual = portions_of(amount, rows * top, most, skew, True), portions_of(amount, rows * top, most, skew, False)
    places = jnp.arange(amount)

    def named(lengths, offset_by):
        used = int((lengths > 0).sum())
        fixed = max(1, used // 4)
        shifted = fixed + (places - fixed + offset_by * (used - fixed)) % max(1, amount - fixed)
        return jnp.zeros((amount,), jnp.int32).at[sequence[jnp.where(places < fixed, places, shifted)]].set(jnp.asarray(lengths, jnp.int32))

    lengths = jnp.where(number % 4 == 0, named(packed, number // 4), named(usual, number - number // 4 - 1))
    mixed = jax.random.permutation(jax.random.fold_in(own, 3), amount)
    giver, sink = mixed[0:amount // 2 * 2:2], mixed[1:amount // 2 * 2:2]
    slack = jnp.minimum(lengths[giver] - 1, most - lengths[sink]) // 2
    slack = jnp.where((giver == sequence[0]) | (sink == sequence[0]) | (lengths[sink] == 0), 0, jnp.maximum(slack, 0))
    shifted = jax.random.randint(jax.random.fold_in(own, 4), (amount // 2,), 0, 1 << 20) % (slack + 1)
    lengths = lengths.at[giver].add(-shifted).at[sink].add(shifted)
    members = jnp.searchsorted(jnp.cumsum(lengths), jnp.arange(rows * top), side="right").astype(jnp.int32)
    grid = members.reshape(top, rows).T
    grid = grid[jax.random.permutation(jax.random.fold_in(own, 1), rows)]
    offset_by = jax.random.randint(jax.random.fold_in(own, 2), (rows, 1), 0, top)
    return jnp.take_along_axis(grid, (jnp.arange(top)[None, :] + offset_by) % top, axis=1)


def portions_of(count, total, reach, skew, full):
    loads = [(1 << 20) // math.isqrt(rank ** skew) + 1 for rank in range(1, count + 1)]
    largest = reach if full else min(reach, max(-(-total // count), total * loads[0] // sum(loads)))
    least = 1 if total - largest >= count - 1 else 0
    holding, spare = [largest] + [least] * (count - 1), total - largest - least * (count - 1)
    while spare > 0:
        free = [i for i in range(1, count) if holding[i] < largest] or [i for i in range(1, count) if holding[i] < reach]
        pool, left = sum([loads[i] for i in free]), spare
        for i in free:
            extra = min(reach - holding[i], max(1, left * loads[i] // pool), spare)
            holding[i] = holding[i] + extra
            spare = spare - extra
    return np.array(holding)


def bell_draw(key, dims, scale, limit, shards=(), kind=jnp.bfloat16):
    values = jax.random.normal(key, dims, jnp.float32) * scale
    if len(shards) > 0:
        values = block_scale(key, dims, shards, -0.22, 0.18) * values
    return jnp.clip(values, min=-limit, max=limit).astype(kind)


def setup_inputs(seed: int = 0) -> dict:
    arg_keys = jax.random.split(jax.random.key(seed), 6)
    trace_values = bell_draw(arg_keys[0], (N_SRC, TRACES, 2 * RB), 1.0, 6.0, ((0, 8), (1, 4)))
    trace_owner_keys = jax.random.split(jax.random.fold_in(arg_keys[1], 1), N_SRC * TRACES // TR_DEV)
    trace_owner_turns = jax.random.permutation(jax.random.fold_in(arg_keys[1], 3), N_SRC * TRACES // TR_DEV)
    trace_owner = jax.vmap(lambda own, number: assign_block(jax.random.fold_in(arg_keys[1], 2), own, number, TR_DEV, N_SLAB, 1, CAP, 2))(trace_owner_keys, trace_owner_turns).reshape((N_SRC, TRACES, 1))
    trace_source = set_ends(jax.random.randint(arg_keys[2], (N_SRC, TRACES), 0, S_DEV), jax.random.fold_in(arg_keys[2], 1), 0, S_DEV - 1).astype(jnp.int32)
    source_fields = bell_draw(arg_keys[3], (2, NSRC, M), (4 * NSRC) ** -0.5, 0.0625, ((1, 4), (2, 8)))
    green_fields = bell_draw(arg_keys[4], (2, NREC, M), (4 * NREC) ** -0.5, 0.0625, ((1, 4), (2, 8)))
    return dict(trace_values=trace_values, trace_owner=trace_owner, trace_source=trace_source, source_fields=source_fields, green_fields=green_fields)


def reference(trace_values, trace_owner, trace_source, source_fields, green_fields):
    source = trace_owner[:, :, 0] * S_DEV + trace_source

    def assemble(pair):
        ids, values = pair
        summed = jax.ops.segment_sum(values.astype(jnp.float32), ids, num_segments=NSRC)
        return summed.astype(jnp.bfloat16)

    blocks = lax.map(assemble, (source, trace_values))
    blocks = blocks.reshape(N_SRC, NSRC, 2, RB)
    res_re = jnp.transpose(blocks[:, :, 0, :], (1, 0, 2)).reshape(NSRC, NREC)
    res_im = jnp.transpose(blocks[:, :, 1, :], (1, 0, 2)).reshape(NSRC, NREC)

    def image_block(index):
        offset = (index * M_DEV).astype(jnp.int32)
        green_re = lax.dynamic_slice_in_dim(green_fields[0], offset, M_DEV, 1)
        green_im = lax.dynamic_slice_in_dim(green_fields[1], offset, M_DEV, 1)
        field_re = lax.dynamic_slice_in_dim(source_fields[0], offset, M_DEV, 1)
        field_im = lax.dynamic_slice_in_dim(source_fields[1], offset, M_DEV, 1)
        adj_re = jnp.dot(res_re, green_re, preferred_element_type=jnp.float32) + jnp.dot(res_im, green_im, preferred_element_type=jnp.float32)
        adj_im = jnp.dot(res_re, green_im, preferred_element_type=jnp.float32) - jnp.dot(res_im, green_re, preferred_element_type=jnp.float32)
        return jnp.sum(field_re.astype(jnp.float32) * adj_re - field_im.astype(jnp.float32) * adj_im, axis=0)

    gradient = lax.map(image_block, jnp.arange(N_SRC, dtype=jnp.int32))
    return gradient.reshape(M)
```

```python
import functools

import jax
import jax.numpy as jnp
from jax import lax
from jax.experimental import pallas as pl
from jax.experimental.pallas import tpu as pltpu
from jax.sharding import PartitionSpec as P

AXES = ("slab", "src")
PAD = 16
TILE = 256
VMEM_LIMIT = 40 * 1024 * 1024


def params():
    return pltpu.CompilerParams(vmem_limit_bytes=VMEM_LIMIT)


SMEM_SPEC = pl.BlockSpec(memory_space=pltpu.SMEM)
VMEM_SPEC = pl.BlockSpec(memory_space=pltpu.VMEM)
ANY_SPEC = pl.BlockSpec(memory_space=pl.ANY)


def number(x, c, y, z, n_src):
    return (2 * x + c) * n_src + 2 * z + y


def id_rows(trace_owner, trace_source, sources_here):
    per = sources_here // TILE
    ids = trace_source[0]
    high = trace_owner[0, :, 0] * per + ids // TILE
    rows = jnp.stack([high, ids % TILE])
    return jnp.pad(rows, ((0, PAD - 2), (0, 0))).astype(jnp.bfloat16)


def prep_kernel(place, mine, other, mine_ids, other_ids, own_ref, away_ref):
    rows, width = mine.shape
    quarter = width // 4
    first = place[0] == 0
    for half, (values, ids) in enumerate(((mine, mine_ids), (other, other_ids))):
        spot = pl.ds(half * rows, rows)
        for part in range(2):
            low = values[:, 2 * part * quarter : (2 * part + 1) * quarter]
            high = values[:, (2 * part + 1) * quarter : (2 * part + 2) * quarter]
            lanes = pl.ds(part * quarter, quarter)
            own_ref[spot, lanes] = jnp.where(first, low, high)
            away_ref[spot, lanes] = jnp.where(first, high, low)
    tiles = rows // TILE
    pieces = [
        ids[kind : kind + 1, j * TILE : (j + 1) * TILE]
        for kind in range(2)
        for ids in (mine_ids, other_ids)
        for j in range(tiles)
    ]
    block = jnp.concatenate(
        pieces + [jnp.zeros((PAD - len(pieces), TILE), jnp.bfloat16)], axis=0
    )
    own_ref[2 * rows :, :] = block
    away_ref[2 * rows :, :] = block


def prep(place, mine, other, mine_ids, other_ids):
    rows, width = mine.shape
    shape = jax.ShapeDtypeStruct((2 * rows + PAD, width // 2), jnp.bfloat16)
    return pl.pallas_call(
        prep_kernel,
        name="prep",
        out_shape=(shape, shape),
        in_specs=[SMEM_SPEC] + [VMEM_SPEC] * 4,
        out_specs=(VMEM_SPEC, VMEM_SPEC),
        compiler_params=params(),
    )(place, mine, other, mine_ids, other_ids)


def fetch(which, candidates, target, sem):
    for k, ref in enumerate(candidates):

        @pl.when(which == k)
        def _(ref=ref):
            copy = pltpu.make_async_copy(ref, target, sem)
            copy.start()
            copy.wait()


def assemble(slab, pieces, group):
    traces = pieces[0].shape[0] - PAD
    tiles = traces // TILE
    iota = lax.broadcasted_iota(jnp.int32, (TILE, TILE), 0).astype(jnp.bfloat16)
    out = []
    owner = slab ^ group
    per = 2
    for h in range(per):
        name = (owner * per + h).astype(jnp.float32).astype(jnp.bfloat16)
        total = None
        for piece in pieces:
            masks = []
            for j in range(tiles):
                high = piece[traces + j : traces + j + 1, :]
                low = piece[traces + tiles + j : traces + tiles + j + 1, :]
                wanted = jnp.where(high == name, low, jnp.bfloat16(-1.0))
                masks.append(
                    jnp.where(iota == wanted, jnp.bfloat16(1.0), jnp.bfloat16(0.0))
                )
            mask = jnp.concatenate(masks, axis=1)
            term = jnp.dot(
                mask, piece[:traces, :], preferred_element_type=jnp.float32
            )
            total = term if total is None else total + term
        out.append(total.astype(jnp.bfloat16))
    return jnp.concatenate(out, axis=0)


def residual_kernel(n_a, n_b, place, *refs):
    cand_a, cand_b = refs[:n_a], refs[n_a : n_a + n_b]
    res_ref, piece_a, piece_b, sem = refs[n_a + n_b :]
    fetch(place[1], cand_a, piece_a, sem)
    fetch(place[1], cand_b, piece_b, sem)
    rows = res_ref.shape[0] // 4
    for group in range(4):
        res_ref[group * rows : (group + 1) * rows, :] = assemble(
            place[0], (piece_a, piece_b), group
        )


def residual(place, cand_a, cand_b, sources):
    piece = cand_a[0].shape
    return pl.pallas_call(
        functools.partial(residual_kernel, len(cand_a), len(cand_b)),
        name="residual",
        out_shape=jax.ShapeDtypeStruct((sources, piece[1]), jnp.bfloat16),
        in_specs=[SMEM_SPEC] + [ANY_SPEC] * (len(cand_a) + len(cand_b)),
        out_specs=VMEM_SPEC,
        scratch_shapes=[
            pltpu.VMEM(piece, jnp.bfloat16),
            pltpu.VMEM(piece, jnp.bfloat16),
            pltpu.SemaphoreType.DMA,
        ],
        compiler_params=params(),
        cost_estimate=pl.CostEstimate(
            flops=2 * sources * 2 * piece[0] * piece[1],
            bytes_accessed=6 * piece[0] * piece[1],
            transcendentals=0,
        ),
    )(place, *cand_a, *cand_b)


def correlate(res, fields):
    contract = (((0,), (0,)), ((), ()))
    rows = fields[0].shape[1]
    half = res[0].shape[1] // 2
    real, imag = None, None
    for group, field in enumerate(fields):
        piece = res[group]
        with_real = lax.dot_general(
            piece, field[0], contract, preferred_element_type=jnp.float32
        )
        with_imag = lax.dot_general(
            piece, field[1], contract, preferred_element_type=jnp.float32
        )
        first = with_real[:half] + with_imag[half:]
        second = with_real[half:] - with_imag[:half]
        real = first if real is None else real + first
        imag = second if imag is None else imag + second
    return real, imag


def correlate_kernel(n_res, *refs):
    res, fields, out_ref = refs[:n_res], refs[n_res : n_res + 4], refs[n_res + 4]
    rows = fields[0].shape[1]
    for k, ref in enumerate(res):
        parts = [ref[g * rows : (g + 1) * rows, :] for g in range(4)]
        real, imag = correlate(parts, fields)
        out_ref[k, 0] = real
        out_ref[k, 1] = imag


def correlated(res, fields):
    half, cells = res[0].shape[1] // 2, fields[0].shape[2]
    return pl.pallas_call(
        functools.partial(correlate_kernel, len(res)),
        name="correlate",
        out_shape=jax.ShapeDtypeStruct((len(res), 2, half, cells), jnp.float32),
        in_specs=[VMEM_SPEC] * (len(res) + 4),
        out_specs=VMEM_SPEC,
        compiler_params=params(),
        cost_estimate=pl.CostEstimate(
            flops=len(res) * 8 * res[0].shape[0] * half * cells,
            bytes_accessed=2 * res[0].size * len(res) + 8 * fields[0].size,
            transcendentals=0,
        ),
    )(*res, *fields)


def last_kernel(n_a, place, *refs):
    cand_a, cand_b = refs[:n_a], refs[n_a : 2 * n_a]
    earlier, near, far = refs[2 * n_a : 2 * n_a + 3]
    fields = refs[2 * n_a + 3 : 2 * n_a + 7]
    out_ref, piece_a, piece_b, sem = refs[2 * n_a + 7 :]
    fetch(place[1], cand_a, piece_a, sem)
    fetch(place[1], cand_b, piece_b, sem)
    parts = [assemble(place[0], (piece_a, piece_b), g) for g in range(4)]
    factors = [(earlier[k, 0], earlier[k, 1]) for k in range(3)]
    factors.append(correlate(parts, fields))
    y, away = place[2], place[3]
    half = near.shape[2]
    total = None
    for k, (real, imag) in zip((0, 1, 2, 3), (factors[0], factors[2], factors[1], factors[3])):
        line = y if k < 2 else 1 - y
        in_far = (away ^ (k % 2)) == 1
        green = [
            jnp.where(in_far, far[p, line], near[p, line]).astype(jnp.float32)
            for p in range(2)
        ]
        term = green[0] * real + green[1] * imag
        total = term if total is None else total + term
    out_ref[...] = jnp.sum(total, axis=0, keepdims=True)


def last(place, cand_a, cand_b, earlier, near, far, fields):
    piece = cand_a[0].shape
    cells = fields[0].shape[2]
    n = len(cand_a)
    return pl.pallas_call(
        functools.partial(last_kernel, n),
        name="last",
        out_shape=jax.ShapeDtypeStruct((1, cells), jnp.float32),
        in_specs=[SMEM_SPEC] + [ANY_SPEC] * (2 * n) + [VMEM_SPEC] * 7,
        out_specs=VMEM_SPEC,
        scratch_shapes=[
            pltpu.VMEM(piece, jnp.bfloat16),
            pltpu.VMEM(piece, jnp.bfloat16),
            pltpu.SemaphoreType.DMA,
        ],
        compiler_params=params(),
        cost_estimate=pl.CostEstimate(
            flops=2 * 4 * fields[0].shape[1] * 2 * piece[0] * piece[1],
            bytes_accessed=12 * 1024 * 1024,
            transcendentals=0,
        ),
    )(place, *cand_a, *cand_b, earlier, near, far, *fields)


def paired(n_src, trace_values, trace_owner, trace_source, source_fields, green_fields):
    values = trace_values[0]
    sources_here = source_fields.shape[1]
    slab = lax.axis_index("slab")
    src = lax.axis_index("src")
    x, c = slab // 2, slab % 2
    z, y = src // 2, src % 2
    lines = range(n_src // 2)

    def send(array, moves):
        pairs = [
            (number(*a, n_src), number(*b, n_src)) for a, b in moves
        ]
        return lax.ppermute(array, AXES, pairs)

    everywhere = [
        (a, b, d, e) for a in range(2) for b in range(2) for d in range(2) for e in lines
    ]
    to_core = [((a, b, d, e), (a, 1 - b, d, e)) for a, b, d, e in everywhere]
    to_x = [((a, b, d, e), (1 - a, b, d, e)) for a, b, d, e in everywhere]
    held = [(a, e % 2, d, e) for a in range(2) for d in range(2) for e in lines]

    def along_z(steps):
        return [
            ((a, b, d, e), (a, b, d, f))
            for b, e, f in steps
            for a in range(2)
            for d in range(2)
        ]

    def across_y(spots):
        return [
            ((a, b, d, e), (a, b, 1 - d, e))
            for b, e in spots
            for a in range(2)
            for d in range(2)
        ]

    mine_ids = id_rows(trace_owner, trace_source, sources_here)
    other = send(values, to_core)
    other_ids = send(mine_ids, to_core)
    own, away = prep(jnp.stack([x]).astype(jnp.int32), values, other, mine_ids, other_ids)
    crossed = send(away, [((a, b, d, e), (1 - a, b, d, e)) for a, b, d, e in held])

    field_x = send(source_fields, to_x)
    field_core = send(source_fields, to_core)
    field_far = send(field_x, to_core)
    fields = (source_fields, field_core, field_x, field_far)

    blocks = green_fields.reshape(2, 2, 2, -1, green_fields.shape[2])
    near = lax.dynamic_index_in_dim(blocks, x, 2, keepdims=False)
    far = send(lax.dynamic_index_in_dim(blocks, 1 - x, 2, keepdims=False), to_x)

    def spread(piece):
        z1 = send(piece, along_z([(0, 0, 1), (0, 2, 3), (1, 3, 2), (1, 1, 0)]))
        y1 = send(piece, across_y([(e % 2, e) for e in lines]))
        z2 = send(piece, along_z([(0, 2, 1), (1, 1, 2)]))
        y2 = send(z1, across_y([(1 - e % 2, e) for e in lines]))
        z3 = send(z1, along_z([(0, 1, 2), (1, 2, 1)]))
        z4 = send(z2, along_z([(0, 1, 0), (1, 2, 3)]))
        z5 = send(z3, along_z([(0, 2, 3), (1, 1, 0)]))
        y3 = send(z2, across_y([(0, 1), (1, 2)]))
        y4 = send(z3, across_y([(0, 2), (1, 1)]))
        y5 = send(z4, across_y([(0, 0), (1, 3)]))
        y6 = send(z5, across_y([(0, 3), (1, 0)]))
        return (piece, z1), (y1, y2), (z2, z3, z4, z5), (y3, y4, y5, y6)

    spread_a, spread_b = spread(own), spread(crossed)
    own_here = (c == z % 2)
    first = jnp.where(own_here, 0, 1)
    outer = ((z == 0) & (c == 0)) | ((z == 3) & (c == 1))
    inner = ((z == 2) & (c == 0)) | ((z == 1) & (c == 1))
    middle = ((z == 1) & (c == 0)) | ((z == 2) & (c == 1))
    second = jnp.where(middle, 0, jnp.where(inner, 1, jnp.where(outer, 2, 3)))
    away_flag = jnp.where(z // 2 == x, 0, 1)

    def place(which):
        return jnp.stack([slab, which, y, away_flag]).astype(jnp.int32)

    sources = 4 * sources_here
    res = [
        residual(place(first), spread_a[0], spread_b[0], sources),
        residual(place(first), spread_a[1], spread_b[1], sources),
        residual(place(second), spread_a[2], spread_b[2], sources),
    ]
    earlier = correlated(res, fields)
    partial = last(
        place(second), spread_a[3], spread_b[3], earlier, near, far, fields
    )[0]
    to_both = [((a, b, d, e), (1 - a, 1 - b, d, e)) for a, b, d, e in everywhere]
    here = partial + send(partial, to_core)
    there = send(partial, to_x) + send(partial, to_both)
    return here + there


def gathered(trace_values, trace_owner, trace_source, source_fields, green_fields):
    values = trace_values[0]
    half_width = values.shape[1] // 2
    src_count = lax.axis_size("src")
    sources_here = source_fields.shape[1]
    slab_index = lax.axis_index("slab")
    high = trace_owner[0, :, 0] * (sources_here // 32) + trace_source[0] // 32
    low = trace_source[0] % 32
    per_slab = sources_here // 32
    piece_values = lax.all_gather(values, "slab", axis=0, tiled=True)
    owners = trace_owner[0, :, 0].astype(jnp.bfloat16)
    high_part = (trace_source[0] // 32).astype(jnp.bfloat16)
    low_part = low.astype(jnp.bfloat16)
    piece_ids = lax.all_gather(
        jnp.stack([owners, high_part, low_part]), "slab", axis=1, tiled=True
    )
    ids = jnp.arange(sources_here, dtype=jnp.int32)
    picks = (
        ((ids // 32).astype(jnp.bfloat16)[:, None] == piece_ids[1][None, :])
        & ((ids % 32).astype(jnp.bfloat16)[:, None] == piece_ids[2][None, :])
        & (piece_ids[0][None, :] == slab_index.astype(jnp.bfloat16))
    )
    assembled = jnp.dot(
        picks.astype(jnp.bfloat16), piece_values, preferred_element_type=jnp.float32
    )
    rows = lax.all_gather(assembled.astype(jnp.bfloat16), "src", axis=1, tiled=True)
    split_rows = rows.reshape(sources_here, src_count, 2, half_width)
    res_real = split_rows[:, :, 0, :].reshape(sources_here, src_count * half_width)
    res_imag = split_rows[:, :, 1, :].reshape(sources_here, src_count * half_width)
    green = lax.all_gather(green_fields, "slab", axis=1, tiled=True)
    dot = functools.partial(jnp.dot, preferred_element_type=jnp.float32)
    adj_real = dot(res_real, green[0]) + dot(res_imag, green[1])
    adj_imag = dot(res_real, green[1]) - dot(res_imag, green[0])
    partial = jnp.sum(
        source_fields[0].astype(jnp.float32) * adj_real
        - source_fields[1].astype(jnp.float32) * adj_imag,
        axis=0,
    )
    return lax.psum(partial, "slab")


def solution(mesh):
    in_specs = (
        P("src", "slab", None),
        P("src", "slab", None),
        P("src", "slab"),
        P(None, "slab", "src"),
        P(None, "slab", "src"),
    )
    n_slab, n_src = mesh.shape["slab"], mesh.shape["src"]
    if n_slab == 2 * 2 and n_src == 2 * 4:
        on_device = functools.partial(paired, n_src)
    else:
        on_device = gathered
    return jax.shard_map(
        on_device, mesh=mesh, in_specs=in_specs, out_specs=P("src"), check_vma=False
    )
```

```python
import functools

import jax
import jax.numpy as jnp
import numpy as np
from jax import lax
from jax.experimental import pallas as pl
from jax.experimental.pallas import tpu as pltpu
from jax.sharding import PartitionSpec as P

AXES = ("slab", "src")
PAD = 16
TILE = 256
VMEM_LIMIT = 24 * 1024 * 1024


def params():
    return pltpu.CompilerParams(vmem_limit_bytes=VMEM_LIMIT)


def light():
    return pl.CostEstimate(flops=1000, bytes_accessed=1000, transcendentals=0)


SMEM_SPEC = pl.BlockSpec(memory_space=pltpu.SMEM)
VMEM_SPEC = pl.BlockSpec(memory_space=pltpu.VMEM)


def number(x, c, y, z, n_src):
    return (2 * x + c) * n_src + 2 * z + y


def id_rows(trace_owner, trace_source, sources_here):
    per = sources_here // TILE
    ids = trace_source[0]
    high = trace_owner[0, :, 0] * per + ids // TILE
    rows = jnp.stack([high, ids % TILE])
    return jnp.pad(rows, ((0, PAD - 2), (0, 0))).astype(jnp.bfloat16)


def id_block(ids, kinds):
    pieces = [
        rows[kind : kind + 1, j * TILE : (j + 1) * TILE]
        for kind in kinds
        for rows in ids
        for j in range(rows.shape[1] // TILE)
    ]
    pad = jnp.zeros((PAD - len(pieces), TILE), jnp.bfloat16)
    return jnp.concatenate(pieces + [pad], axis=0)


def receivers(values, first, rows, out_ref, spot):
    quarter = values.shape[1] // 4
    for part in range(2):
        low = values[:, 2 * part * quarter : (2 * part + 1) * quarter]
        high = values[:, (2 * part + 1) * quarter : (2 * part + 2) * quarter]
        lanes = pl.ds(part * quarter, quarter)
        out_ref[pl.ds(spot, rows), lanes] = jnp.where(first, low, high)


def cut_kernel(n, place, *refs):
    values, ids, out_ref = refs[:n], refs[n : 2 * n], refs[2 * n]
    rows = values[0].shape[0]
    for k, ref in enumerate(values):
        receivers(ref, place[0] == 0, rows, out_ref, k * rows)
    out_ref[n * rows :, :] = id_block(ids, range(2))


def cut(half, values, ids):
    rows, width = values[0].shape
    n = len(values)
    return pl.pallas_call(
        functools.partial(cut_kernel, n),
        name="cut",
        out_shape=jax.ShapeDtypeStruct((n * rows + PAD, width // 2), jnp.bfloat16),
        in_specs=[SMEM_SPEC] + [VMEM_SPEC] * (2 * n),
        out_specs=VMEM_SPEC,
        compiler_params=params(),
        cost_estimate=light(),
    )(half, *values, *ids)


def pick_kernel(n, place, *refs):
    fetch(place[0], refs[:n], refs[n], refs[n + 1])


def pick(which, candidates):
    first = candidates[0]
    return pl.pallas_call(
        functools.partial(pick_kernel, len(candidates)),
        name="pick",
        out_shape=jax.ShapeDtypeStruct(first.shape, first.dtype),
        in_specs=[SMEM_SPEC] + [VMEM_SPEC] * len(candidates),
        out_specs=VMEM_SPEC,
        scratch_shapes=[pltpu.SemaphoreType.DMA],
        compiler_params=params(),
        cost_estimate=light(),
    )(which, *candidates)


def join_kernel(mine, other, out_ref):
    rows = mine.shape[0] - PAD
    tiles = rows // TILE
    out_ref[:rows, :] = mine[:rows, :]
    out_ref[rows : 2 * rows, :] = other[:rows, :]
    ids = [mine[rows:, :], other[rows:, :]]
    pieces = [part[kind * tiles : (kind + 1) * tiles] for kind in range(2) for part in ids]
    pad = jnp.zeros((PAD - 4 * tiles, TILE), jnp.bfloat16)
    out_ref[2 * rows :, :] = jnp.concatenate(pieces + [pad], axis=0)


def join(mine, other):
    rows, width = mine.shape
    return pl.pallas_call(
        join_kernel,
        name="join",
        out_shape=jax.ShapeDtypeStruct((2 * rows - PAD, width), jnp.bfloat16),
        in_specs=[VMEM_SPEC] * 2,
        out_specs=VMEM_SPEC,
        compiler_params=params(),
        cost_estimate=light(),
    )(mine, other)


def halves_kernel(place, blocks, near_ref, away_ref):
    first = place[0] == 0
    for p in range(blocks.shape[0]):
        for line in range(blocks.shape[1]):
            low, high = blocks[p, line, 0], blocks[p, line, 1]
            near_ref[p, line] = jnp.where(first, low, high)
            away_ref[p, line] = jnp.where(first, high, low)


def halves(place, blocks):
    shape = jax.ShapeDtypeStruct(blocks.shape[:2] + blocks.shape[3:], blocks.dtype)
    return pl.pallas_call(
        halves_kernel,
        name="halves",
        out_shape=(shape, shape),
        in_specs=[SMEM_SPEC, VMEM_SPEC],
        out_specs=(VMEM_SPEC, VMEM_SPEC),
        compiler_params=params(),
        cost_estimate=light(),
    )(place, blocks)


def fetch(which, candidates, target, sem):
    for k, ref in enumerate(candidates):

        @pl.when(which == k)
        def _(ref=ref):
            copy = pltpu.make_async_copy(ref, target, sem)
            copy.start()
            copy.wait()


def assemble(slab, pieces, group, start=None):
    traces = pieces[0].shape[0] - PAD
    tiles = traces // TILE
    iota = lax.broadcasted_iota(jnp.int32, (TILE, TILE), 0).astype(jnp.bfloat16)
    out = []
    owner = slab ^ group
    per = 2
    for h in range(per):
        name = (owner * per + h).astype(jnp.float32).astype(jnp.bfloat16)
        total = None if start is None else start[h * TILE : (h + 1) * TILE, :]
        for piece in pieces:
            masks = []
            for j in range(tiles):
                high = piece[traces + j : traces + j + 1, :]
                low = piece[traces + tiles + j : traces + tiles + j + 1, :]
                wanted = jnp.where(high == name, low, jnp.bfloat16(-1.0))
                masks.append(
                    jnp.where(iota == wanted, jnp.bfloat16(1.0), jnp.bfloat16(0.0))
                )
            mask = jnp.concatenate(masks, axis=1)
            term = jnp.dot(
                mask, piece[:traces, :], preferred_element_type=jnp.float32
            )
            total = term if total is None else total + term
        out.append(total)
    return jnp.concatenate(out, axis=0)


def residual_kernel(n, place, *refs):
    out_ref = refs[n]
    rows = out_ref.shape[0] // 4
    for group in range(4):
        out_ref[group * rows : (group + 1) * rows, :] = assemble(
            place[0], refs[:n], group
        ).astype(out_ref.dtype)


def residual(place, pieces, sources, dtype=jnp.bfloat16):
    return pl.pallas_call(
        functools.partial(residual_kernel, len(pieces)),
        name="residual",
        out_shape=jax.ShapeDtypeStruct((sources, pieces[0].shape[1]), dtype),
        in_specs=[SMEM_SPEC] + [VMEM_SPEC] * len(pieces),
        out_specs=VMEM_SPEC,
        compiler_params=params(),
        cost_estimate=light(),
    )(place, *pieces)


def correlate(res, fields):
    contract = (((0,), (0,)), ((), ()))
    dot = functools.partial(
        lax.dot_general,
        dimension_numbers=contract,
        preferred_element_type=jnp.float32,
    )
    half = res[0].shape[1] // 2
    real, imag = None, None
    for piece, field in zip(res, fields):
        with_real, with_imag = dot(piece, field[0]), dot(piece, field[1])
        first = with_real[:half] + with_imag[half:]
        second = with_real[half:] - with_imag[:half]
        real = first if real is None else real + first
        imag = second if imag is None else imag + second
    return real, imag


def correlate_kernel(n_res, *refs):
    res, out_ref = refs[:n_res], refs[-1]
    fields = refs[n_res:-1]
    rows = res[0].shape[0] // 4
    for k, ref in enumerate(res):
        parts = [ref[g * rows : (g + 1) * rows, :] for g in range(4)]
        real, imag = correlate(parts, fields)
        out_ref[k, 0] = real
        out_ref[k, 1] = imag


def correlated(res, fields):
    half, cells = res[0].shape[1] // 2, fields[0].shape[2]
    return pl.pallas_call(
        functools.partial(correlate_kernel, len(res)),
        name="correlate",
        out_shape=jax.ShapeDtypeStruct((len(res), 2, half, cells), jnp.float32),
        in_specs=[VMEM_SPEC] * (len(res) + len(fields)),
        out_specs=VMEM_SPEC,
        compiler_params=params(),
        cost_estimate=light(),
    )(*res, *fields)


def fetch_green(place, slot, greens, target, sems):
    group, line = place[1 + 2 * slot], place[2 + 2 * slot]
    for j, ref in enumerate(greens):

        @pl.when(group == j)
        def _(ref=ref):
            for p in range(2):
                pltpu.make_async_copy(ref.at[p, line], target.at[p], sems.at[p]).start()

    def wait():
        for p in range(2):
            pltpu.make_async_copy(greens[0].at[p, 0], target.at[p], sems.at[p]).wait()

    return wait


def fold_kernel(place, factors, *refs):
    greens, (out_ref, green, sems) = refs[:4], refs[4:]
    slots = factors.shape[0]
    waits = [
        fetch_green(place, k, greens, green.at[k], sems.at[k]) for k in range(slots)
    ]
    total = None
    for k in range(slots):
        waits[k]()
        for p in range(2):
            term = green[k, p].astype(jnp.float32) * factors[k, p]
            total = term if total is None else total + term
    out_ref[...] = jnp.sum(total, axis=0, keepdims=True)


def fold(place, factors, greens):
    slots = factors.shape[0]
    return pl.pallas_call(
        fold_kernel,
        name="fold",
        out_shape=jax.ShapeDtypeStruct((1, factors.shape[3]), jnp.float32),
        in_specs=[SMEM_SPEC] + [VMEM_SPEC] * (1 + len(greens)),
        out_specs=VMEM_SPEC,
        scratch_shapes=[
            pltpu.VMEM((slots, 2) + greens[0].shape[2:], jnp.bfloat16),
            pltpu.SemaphoreType.DMA((slots, 2)),
        ],
        compiler_params=params(),
        cost_estimate=light(),
    )(place, factors, *greens)


def last_kernel(n_b, place, *refs):
    cand_b, (begun, folded) = refs[:n_b], refs[n_b : n_b + 2]
    greens, fields = refs[n_b + 2 : n_b + 6], refs[n_b + 6 : n_b + 10]
    out_ref, piece, green, sem, sems = refs[n_b + 10 :]
    wait = fetch_green(place, 3, greens, green, sems)
    fetch(place[9], cand_b, piece, sem)
    rows = begun.shape[0] // 4
    parts = [
        assemble(
            place[0], (piece,), g, begun[g * rows : (g + 1) * rows, :]
        ).astype(jnp.bfloat16)
        for g in range(4)
    ]
    real, imag = correlate(parts, fields)
    wait()
    total = green[0].astype(jnp.float32) * real + green[1].astype(jnp.float32) * imag
    out_ref[...] = folded[...] + jnp.sum(total, axis=0, keepdims=True)


def last(place, cand_b, begun, folded, greens, fields):
    return pl.pallas_call(
        functools.partial(last_kernel, len(cand_b)),
        name="last",
        out_shape=jax.ShapeDtypeStruct(folded.shape, jnp.float32),
        in_specs=[SMEM_SPEC]
        + [VMEM_SPEC] * (len(cand_b) + 2 + len(greens) + len(fields)),
        out_specs=VMEM_SPEC,
        scratch_shapes=[
            pltpu.VMEM(cand_b[0].shape, jnp.bfloat16),
            pltpu.VMEM((2,) + greens[0].shape[2:], jnp.bfloat16),
            pltpu.SemaphoreType.DMA,
            pltpu.SemaphoreType.DMA((2,)),
        ],
        compiler_params=params(),
        cost_estimate=light(),
    )(place, *cand_b, begun, folded, *greens, *fields)


def paired(n_src, trace_values, trace_owner, trace_source, source_fields, green_fields):
    values = trace_values[0]
    sources_here = source_fields.shape[1]
    slab = lax.axis_index("slab")
    src = lax.axis_index("src")
    x, c = slab // 2, slab % 2
    z, y = src // 2, src % 2
    lines = range(n_src // 2)

    def send(array, moves):
        pairs = [
            (number(*a, n_src), number(*b, n_src)) for a, b in moves
        ]
        return lax.ppermute(array, AXES, pairs)

    everywhere = [
        (a, b, d, e) for a in range(2) for b in range(2) for d in range(2) for e in lines
    ]
    to_core = [((a, b, d, e), (a, 1 - b, d, e)) for a, b, d, e in everywhere]
    to_x = [((a, b, d, e), (1 - a, b, d, e)) for a, b, d, e in everywhere]
    to_both = [((a, b, d, e), (1 - a, 1 - b, d, e)) for a, b, d, e in everywhere]

    def after(array, *earlier):
        return lax.optimization_barrier((array, *earlier))[0]

    other = send(values, to_core)
    mine_ids = id_rows(trace_owner, trace_source, sources_here)
    other_ids = send(mine_ids, to_core)
    place_x = jnp.stack([x]).astype(jnp.int32)
    crossed_here = send(cut(1 - place_x, (values,), (mine_ids,)), to_x)
    own = cut(place_x, (values, other), (mine_ids, other_ids))
    crossed = join(crossed_here, send(crossed_here, to_core))

    moves = []
    for steps in (
        [(0, 0, 1, None), (1, 0, 0, 1), (0, 1, 0, 0), (1, 1, 1, 2)],
        [(0, 0, 1, None), (1, 1, 0, 0), (0, 1, 0, 2)],
        [(0, 0, 1, None), (1, 0, 0, 1), (0, 1, 0, 0), (1, 1, 1, None)],
        [(0, 0, 1, None), (1, 0, 0, 1), (0, 1, 1, None)],
    ):
        pairs = []
        for here_c, here_z, there_c, there_z in steps:
            for a in range(2):
                for d in range(2):
                    for e in (here_z, len(lines) - 1 - here_z):
                        if there_z is None:
                            target = (a, there_c, 1 - d, e)
                        else:
                            far_z = there_z if e == here_z else len(lines) - 1 - there_z
                            target = (a, there_c, d, far_z)
                        pairs.append(((a, here_c, d, e), target))
        moves.append(pairs)
    brought = np.array(
        [
            [[(1, 0), (2, 0), (3, 0), (0, 0)], [(0, 1), (1, 1), (2, 1), (3, 1)]],
            [[(0, 0), (3, 0), (0, 1), (1, 1)], [(2, 0), (1, 0), (2, 1), (3, 1)]],
        ],
        np.int32,
    )
    mirrored = brought[::-1].copy()
    mirrored[..., 0] = len(lines) - 1 - mirrored[..., 0]
    table = jnp.asarray(np.concatenate([brought, mirrored]))
    outer = (z == 0) | (z == len(lines) - 1)

    mine_now = lax.dynamic_index_in_dim(
        lax.dynamic_index_in_dim(table, z, 0, keepdims=False), c, 0, keepdims=False
    )
    groups = jnp.bitwise_xor(mine_now[:, 0], slab)
    on_line = jnp.bitwise_xor(mine_now[:, 1], y)
    where_green = jnp.stack([groups, on_line], axis=1).reshape(-1)
    stay_2 = jnp.where((~outer) & (c == 1), 1, 0)
    stay_4 = jnp.where(outer & (c == 0), 1, 0)
    place = jnp.concatenate(
        [jnp.stack([slab]), where_green, jnp.stack([stay_4])]
    ).astype(jnp.int32)
    stay_2, stay_4 = (jnp.stack([k]).astype(jnp.int32) for k in (stay_2, stay_4))
    core = jnp.stack([c]).astype(jnp.int32)
    sources = 4 * sources_here

    r1_a = send(own, moves[0])
    r2_a = send(r1_a, moves[1])
    r1_b = send(after(crossed, r1_a), moves[0])
    r3_a = send(pick(core, (r2_a, r1_a)), moves[2])
    r2_b = send(after(r1_b, r2_a), moves[1])
    res_1 = residual(place, (r1_a, after(r1_b, r2_a)), sources)
    r4_a = send(pick(1 - stay_4, (after(r3_a, res_1), r2_a)), moves[3])
    to_r3_b = pick(core, (after(r2_b, r3_a), r1_b))
    r3_b = send(to_r3_b, moves[2])
    second_a, second_b = pick(stay_2, (r2_a, own)), pick(stay_2, (r2_b, crossed))
    res_2 = residual(place, (second_a, after(second_b, to_r3_b)), sources)
    fourth_a = pick(stay_4, (after(r4_a, res_2), own))
    to_r4_b = pick(1 - stay_4, (after(r3_b, fourth_a), r2_b))
    r4_b = send(to_r4_b, moves[3])

    field_core = send(after(source_fields, own), to_core)
    field_x = send(after(source_fields, crossed_here), to_x)
    field_far = send(after(field_x, to_r3_b), to_core)
    fields = (source_fields, field_core, field_x, field_far)

    blocks = green_fields.reshape(2, 2, 2, -1, green_fields.shape[2])
    near, away_green = halves(place_x, after(blocks, r1_a))
    far = send(after(away_green, r2_a), to_x)
    far_core = send(after(far, to_r4_b), to_core)
    greens = (near, send(near, to_core), far, far_core)

    res_3 = residual(place, (r3_a, after(r3_b, to_r4_b)), sources)
    factors = correlated((res_1, res_2, res_3), fields)
    begun = residual(place, (fourth_a,), sources, jnp.float32)
    folded = fold(place, factors, greens)
    partial = last(place, (r4_b, crossed), begun, folded, greens, fields)[0]
    here = partial + send(partial, to_core)
    there = send(partial, to_x) + send(partial, to_both)
    return here + there


def gathered(trace_values, trace_owner, trace_source, source_fields, green_fields):
    values = trace_values[0]
    half_width = values.shape[1] // 2
    src_count = lax.axis_size("src")
    sources_here = source_fields.shape[1]
    slab_index = lax.axis_index("slab")
    high = trace_owner[0, :, 0] * (sources_here // 32) + trace_source[0] // 32
    low = trace_source[0] % 32
    per_slab = sources_here // 32
    piece_values = lax.all_gather(values, "slab", axis=0, tiled=True)
    owners = trace_owner[0, :, 0].astype(jnp.bfloat16)
    high_part = (trace_source[0] // 32).astype(jnp.bfloat16)
    low_part = low.astype(jnp.bfloat16)
    piece_ids = lax.all_gather(
        jnp.stack([owners, high_part, low_part]), "slab", axis=1, tiled=True
    )
    ids = jnp.arange(sources_here, dtype=jnp.int32)
    picks = (
        ((ids // 32).astype(jnp.bfloat16)[:, None] == piece_ids[1][None, :])
        & ((ids % 32).astype(jnp.bfloat16)[:, None] == piece_ids[2][None, :])
        & (piece_ids[0][None, :] == slab_index.astype(jnp.bfloat16))
    )
    assembled = jnp.dot(
        picks.astype(jnp.bfloat16), piece_values, preferred_element_type=jnp.float32
    )
    rows = lax.all_gather(assembled.astype(jnp.bfloat16), "src", axis=1, tiled=True)
    split_rows = rows.reshape(sources_here, src_count, 2, half_width)
    res_real = split_rows[:, :, 0, :].reshape(sources_here, src_count * half_width)
    res_imag = split_rows[:, :, 1, :].reshape(sources_here, src_count * half_width)
    green = lax.all_gather(green_fields, "slab", axis=1, tiled=True)
    dot = functools.partial(jnp.dot, preferred_element_type=jnp.float32)
    adj_real = dot(res_real, green[0]) + dot(res_imag, green[1])
    adj_imag = dot(res_real, green[1]) - dot(res_imag, green[0])
    partial = jnp.sum(
        source_fields[0].astype(jnp.float32) * adj_real
        - source_fields[1].astype(jnp.float32) * adj_imag,
        axis=0,
    )
    return lax.psum(partial, "slab")


def solution(mesh):
    in_specs = (
        P("src", "slab", None),
        P("src", "slab", None),
        P("src", "slab"),
        P(None, "slab", "src"),
        P(None, "slab", "src"),
    )
    n_slab, n_src = mesh.shape["slab"], mesh.shape["src"]
    if n_slab == 2 * 2 and n_src == 2 * 4:
        on_device = functools.partial(paired, n_src)
    else:
        on_device = gathered
    return jax.shard_map(
        on_device, mesh=mesh, in_specs=in_specs, out_specs=P("src"), check_vma=False
    )
```

```python
import functools

import jax
import jax.numpy as jnp
import numpy as np
from jax import lax
from jax.experimental import pallas as pl
from jax.experimental.pallas import tpu as pltpu
from jax.sharding import PartitionSpec as P

AXES = ("slab", "src")
PAD = 16
TILE = 256
VMEM_LIMIT = 24 * 1024 * 1024


def params():
    return pltpu.CompilerParams(vmem_limit_bytes=VMEM_LIMIT)


def light():
    return pl.CostEstimate(flops=1000, bytes_accessed=1000, transcendentals=0)


SMEM_SPEC = pl.BlockSpec(memory_space=pltpu.SMEM)
VMEM_SPEC = pl.BlockSpec(memory_space=pltpu.VMEM)


def number(x, c, y, z, n_src):
    return (2 * x + c) * n_src + 2 * z + y


def id_rows(trace_owner, trace_source, sources_here):
    per = sources_here // TILE
    ids = trace_source[0]
    high = trace_owner[0, :, 0] * per + ids // TILE
    rows = jnp.stack([high, ids % TILE])
    return jnp.pad(rows, ((0, PAD - 2), (0, 0))).astype(jnp.bfloat16)


def id_block(ids, kinds):
    pieces = [
        rows[kind : kind + 1, j * TILE : (j + 1) * TILE]
        for kind in kinds
        for rows in ids
        for j in range(rows.shape[1] // TILE)
    ]
    pad = jnp.zeros((PAD - len(pieces), TILE), jnp.bfloat16)
    return jnp.concatenate(pieces + [pad], axis=0)


def receivers(values, first, rows, out_ref, spot):
    quarter = values.shape[1] // 4
    for part in range(2):
        low = values[:, 2 * part * quarter : (2 * part + 1) * quarter]
        high = values[:, (2 * part + 1) * quarter : (2 * part + 2) * quarter]
        lanes = pl.ds(part * quarter, quarter)
        out_ref[pl.ds(spot, rows), lanes] = jnp.where(first, low, high)


def cut_kernel(n, place, *refs):
    values, ids, (out_ref, mine, sem) = refs[:n], refs[n : 2 * n], refs[2 * n :]
    copy = pltpu.make_async_copy(values[0], mine, sem)
    copy.start()
    rows = mine.shape[0]
    out_ref[n * rows :, :] = id_block(ids, range(2))
    for k in range(1, n):
        receivers(values[k], place[0] == 0, rows, out_ref, k * rows)
    copy.wait()
    receivers(mine, place[0] == 0, rows, out_ref, 0)


def cut(half, values, ids):
    rows, width = values[0].shape
    n = len(values)
    return pl.pallas_call(
        functools.partial(cut_kernel, n),
        name="cut",
        out_shape=jax.ShapeDtypeStruct((n * rows + PAD, width // 2), jnp.bfloat16),
        in_specs=[SMEM_SPEC, pl.BlockSpec(memory_space=pltpu.HBM)]
        + [VMEM_SPEC] * (2 * n - 1),
        out_specs=VMEM_SPEC,
        scratch_shapes=[
            pltpu.VMEM(values[0].shape, jnp.bfloat16),
            pltpu.SemaphoreType.DMA,
        ],
        compiler_params=params(),
        cost_estimate=light(),
    )(half, *values, *ids)


def join_kernel(mine, other, out_ref):
    rows = mine.shape[0] - PAD
    tiles = rows // TILE
    out_ref[:rows, :] = mine[:rows, :]
    out_ref[rows : 2 * rows, :] = other[:rows, :]
    ids = [mine[rows:, :], other[rows:, :]]
    pieces = [part[kind * tiles : (kind + 1) * tiles] for kind in range(2) for part in ids]
    pad = jnp.zeros((PAD - 4 * tiles, TILE), jnp.bfloat16)
    out_ref[2 * rows :, :] = jnp.concatenate(pieces + [pad], axis=0)


def join(mine, other):
    rows, width = mine.shape
    return pl.pallas_call(
        join_kernel,
        name="join",
        out_shape=jax.ShapeDtypeStruct((2 * rows - PAD, width), jnp.bfloat16),
        in_specs=[VMEM_SPEC] * 2,
        out_specs=VMEM_SPEC,
        compiler_params=params(),
        cost_estimate=light(),
    )(mine, other)


def halves_kernel(place, blocks, near_ref, away_ref):
    first = place[0] == 0
    for p in range(blocks.shape[0]):
        for line in range(blocks.shape[1]):
            low, high = blocks[p, line, 0], blocks[p, line, 1]
            near_ref[p, line] = jnp.where(first, low, high)
            away_ref[p, line] = jnp.where(first, high, low)


def halves(place, blocks):
    shape = jax.ShapeDtypeStruct(blocks.shape[:2] + blocks.shape[3:], blocks.dtype)
    return pl.pallas_call(
        halves_kernel,
        name="halves",
        out_shape=(shape, shape),
        in_specs=[SMEM_SPEC, VMEM_SPEC],
        out_specs=(VMEM_SPEC, VMEM_SPEC),
        compiler_params=params(),
        cost_estimate=light(),
    )(place, blocks)


def fetch(which, candidates, target, sem):
    for k, ref in enumerate(candidates):

        @pl.when(which == k)
        def _(ref=ref):
            copy = pltpu.make_async_copy(ref, target, sem)
            copy.start()
            copy.wait()


def assemble(slab, pieces, group, start=None):
    traces = pieces[0].shape[0] - PAD
    tiles = traces // TILE
    iota = lax.broadcasted_iota(jnp.int32, (TILE, TILE), 0).astype(jnp.bfloat16)
    out = []
    owner = slab ^ group
    per = 2
    for h in range(per):
        name = (owner * per + h).astype(jnp.float32).astype(jnp.bfloat16)
        total = None if start is None else start[h * TILE : (h + 1) * TILE, :]
        for piece in pieces:
            masks = []
            for j in range(tiles):
                high = piece[traces + j : traces + j + 1, :]
                low = piece[traces + tiles + j : traces + tiles + j + 1, :]
                wanted = jnp.where(high == name, low, jnp.bfloat16(-1.0))
                masks.append(
                    jnp.where(iota == wanted, jnp.bfloat16(1.0), jnp.bfloat16(0.0))
                )
            mask = jnp.concatenate(masks, axis=1)
            term = jnp.dot(
                mask, piece[:traces, :], preferred_element_type=jnp.float32
            )
            total = term if total is None else total + term
        out.append(total)
    return jnp.concatenate(out, axis=0)


def residual_kernel(n, place, *refs):
    out_ref = refs[n]
    rows = out_ref.shape[0] // 4
    for group in range(4):
        out_ref[group * rows : (group + 1) * rows, :] = assemble(
            place[0], refs[:n], group
        ).astype(out_ref.dtype)


def residual(place, pieces, sources):
    return pl.pallas_call(
        functools.partial(residual_kernel, len(pieces)),
        name="residual",
        out_shape=jax.ShapeDtypeStruct((sources, pieces[0].shape[1]), jnp.bfloat16),
        in_specs=[SMEM_SPEC] + [VMEM_SPEC] * len(pieces),
        out_specs=VMEM_SPEC,
        compiler_params=params(),
        cost_estimate=light(),
    )(place, *pieces)


def begin_kernel(n, place, *refs):
    cand, (out_ref, piece, sem) = refs[:n], refs[n:]
    fetch(place[9], cand, piece, sem)
    rows = out_ref.shape[0] // 4
    for group in range(4):
        out_ref[group * rows : (group + 1) * rows, :] = assemble(
            place[0], (piece,), group
        )


def begin(place, cand, sources):
    shape = cand[0].shape
    return pl.pallas_call(
        functools.partial(begin_kernel, len(cand)),
        name="begin",
        out_shape=jax.ShapeDtypeStruct((sources, shape[1]), jnp.float32),
        in_specs=[SMEM_SPEC] + [VMEM_SPEC] * len(cand),
        out_specs=VMEM_SPEC,
        scratch_shapes=[pltpu.VMEM(shape, jnp.bfloat16), pltpu.SemaphoreType.DMA],
        compiler_params=params(),
        cost_estimate=light(),
    )(place, *cand)


def correlate(res, fields):
    contract = (((0,), (0,)), ((), ()))
    dot = functools.partial(
        lax.dot_general,
        dimension_numbers=contract,
        preferred_element_type=jnp.float32,
    )
    half = res[0].shape[1] // 2
    real, imag = None, None
    for piece, field in zip(res, fields):
        with_real, with_imag = dot(piece, field[0]), dot(piece, field[1])
        first = with_real[:half] + with_imag[half:]
        second = with_real[half:] - with_imag[:half]
        real = first if real is None else real + first
        imag = second if imag is None else imag + second
    return real, imag


def correlate_kernel(n_res, *refs):
    res, out_ref = refs[:n_res], refs[-1]
    fields = refs[n_res:-1]
    rows = res[0].shape[0] // 4
    for k, ref in enumerate(res):
        parts = [ref[g * rows : (g + 1) * rows, :] for g in range(4)]
        real, imag = correlate(parts, fields)
        out_ref[k, 0] = real
        out_ref[k, 1] = imag


def correlated(res, fields):
    half, cells = res[0].shape[1] // 2, fields[0].shape[2]
    return pl.pallas_call(
        functools.partial(correlate_kernel, len(res)),
        name="correlate",
        out_shape=jax.ShapeDtypeStruct((len(res), 2, half, cells), jnp.float32),
        in_specs=[VMEM_SPEC] * (len(res) + len(fields)),
        out_specs=VMEM_SPEC,
        compiler_params=params(),
        cost_estimate=light(),
    )(*res, *fields)


def fetch_green(place, slot, greens, target, sems):
    group, line = place[1 + 2 * slot], place[2 + 2 * slot]
    for j, ref in enumerate(greens):

        @pl.when(group == j)
        def _(ref=ref):
            for p in range(2):
                pltpu.make_async_copy(ref.at[p, line], target.at[p], sems.at[p]).start()

    def wait():
        for p in range(2):
            pltpu.make_async_copy(greens[0].at[p, 0], target.at[p], sems.at[p]).wait()

    return wait


def fold_kernel(n, place, *refs):
    factors, greens, (out_ref, green, sems) = refs[:n], refs[n : n + 4], refs[n + 4 :]
    slots = [(ref, k) for ref in factors for k in range(ref.shape[0])]
    waits = [
        fetch_green(place, j, greens, green.at[j], sems.at[j])
        for j in range(len(slots))
    ]
    total = None
    for j, (ref, k) in enumerate(slots):
        waits[j]()
        for p in range(2):
            term = green[j, p].astype(jnp.float32) * ref[k, p]
            total = term if total is None else total + term
    out_ref[...] = jnp.sum(total, axis=0, keepdims=True)


def fold(place, factors, greens):
    slots = sum(f.shape[0] for f in factors)
    return pl.pallas_call(
        functools.partial(fold_kernel, len(factors)),
        name="fold",
        out_shape=jax.ShapeDtypeStruct((1, factors[0].shape[3]), jnp.float32),
        in_specs=[SMEM_SPEC] + [VMEM_SPEC] * (len(factors) + len(greens)),
        out_specs=VMEM_SPEC,
        scratch_shapes=[
            pltpu.VMEM((slots, 2) + greens[0].shape[2:], jnp.bfloat16),
            pltpu.SemaphoreType.DMA((slots, 2)),
        ],
        compiler_params=params(),
        cost_estimate=light(),
    )(place, *factors, *greens)


def last_kernel(n_b, place, *refs):
    cand_b, (begun, folded) = refs[:n_b], refs[n_b : n_b + 2]
    greens, fields = refs[n_b + 2 : n_b + 6], refs[n_b + 6 : n_b + 10]
    out_ref, piece, green, sem, sems = refs[n_b + 10 :]
    wait = fetch_green(place, 3, greens, green, sems)
    fetch(place[9], cand_b, piece, sem)
    rows = begun.shape[0] // 4
    parts = [
        assemble(
            place[0], (piece,), g, begun[g * rows : (g + 1) * rows, :]
        ).astype(jnp.bfloat16)
        for g in range(4)
    ]
    real, imag = correlate(parts, fields)
    wait()
    total = green[0].astype(jnp.float32) * real + green[1].astype(jnp.float32) * imag
    out_ref[...] = folded[...] + jnp.sum(total, axis=0, keepdims=True)


def last(place, cand_b, begun, folded, greens, fields):
    return pl.pallas_call(
        functools.partial(last_kernel, len(cand_b)),
        name="last",
        out_shape=jax.ShapeDtypeStruct(folded.shape, jnp.float32),
        in_specs=[SMEM_SPEC]
        + [VMEM_SPEC] * (len(cand_b) + 2 + len(greens) + len(fields)),
        out_specs=VMEM_SPEC,
        scratch_shapes=[
            pltpu.VMEM(cand_b[0].shape, jnp.bfloat16),
            pltpu.VMEM((2,) + greens[0].shape[2:], jnp.bfloat16),
            pltpu.SemaphoreType.DMA,
            pltpu.SemaphoreType.DMA((2,)),
        ],
        compiler_params=params(),
        cost_estimate=light(),
    )(place, *cand_b, begun, folded, *greens, *fields)


def paired(n_src, trace_values, trace_owner, trace_source, source_fields, green_fields):
    values = trace_values[0]
    sources_here = source_fields.shape[1]
    slab = lax.axis_index("slab")
    src = lax.axis_index("src")
    x, c = slab // 2, slab % 2
    z, y = src // 2, src % 2
    lines = range(n_src // 2)

    def send(array, moves):
        pairs = [
            (number(*a, n_src), number(*b, n_src)) for a, b in moves
        ]
        return lax.ppermute(array, AXES, pairs)

    everywhere = [
        (a, b, d, e) for a in range(2) for b in range(2) for d in range(2) for e in lines
    ]
    to_core = [((a, b, d, e), (a, 1 - b, d, e)) for a, b, d, e in everywhere]
    to_x = [((a, b, d, e), (1 - a, b, d, e)) for a, b, d, e in everywhere]
    to_both = [((a, b, d, e), (1 - a, 1 - b, d, e)) for a, b, d, e in everywhere]

    def after(array, *earlier):
        return lax.optimization_barrier((array, *earlier))[0]

    other = send(values, to_core)
    mine_ids = id_rows(trace_owner, trace_source, sources_here)
    other_ids = send(mine_ids, to_core)
    place_x = jnp.stack([x]).astype(jnp.int32)
    crossed_here = send(cut(1 - place_x, (values,), (mine_ids,)), to_x)
    own = cut(place_x, (values, other), (mine_ids, other_ids))
    crossed = join(crossed_here, send(crossed_here, to_core))

    moves = []
    for steps in (
        [(0, 0, 1, None), (1, 0, 1, 1), (0, 1, 0, 0), (1, 1, 0, 2)],
        [(0, 0, 1, None), (1, 0, 0, 1), (0, 1, 0, 0), (1, 1, 1, 2)],
        [(0, 0, 1, None), (1, 0, 1, 1), (0, 1, 0, 2), (1, 1, 0, 0)],
        [(0, 0, 1, None), (1, 1, 1, 2)],
        [(1, 0, 1, 1), (0, 1, 1, 0)],
    ):
        pairs = []
        for here_c, here_z, there_c, there_z in steps:
            for a in range(2):
                for d in range(2):
                    for e in (here_z, len(lines) - 1 - here_z):
                        if there_z is None:
                            target = (a, there_c, 1 - d, e)
                        else:
                            far_z = there_z if e == here_z else len(lines) - 1 - there_z
                            target = (a, there_c, d, far_z)
                        pairs.append(((a, here_c, d, e), target))
        moves.append(pairs)
    brought = np.array(
        [
            [[(1, 0), (2, 0), (3, 0), (0, 0)], [(0, 1), (1, 1), (2, 1), (3, 1)]],
            [[(2, 0), (0, 1), (3, 1), (1, 0)], [(0, 0), (3, 0), (1, 1), (2, 1)]],
        ],
        np.int32,
    )
    mirrored = brought[::-1].copy()
    mirrored[..., 0] = len(lines) - 1 - mirrored[..., 0]
    table = jnp.asarray(np.concatenate([brought, mirrored]))

    mine_now = lax.dynamic_index_in_dim(
        lax.dynamic_index_in_dim(table, z, 0, keepdims=False), c, 0, keepdims=False
    )
    groups = jnp.bitwise_xor(mine_now[:, 0], slab)
    on_line = jnp.bitwise_xor(mine_now[:, 1], y)
    where_green = jnp.stack([groups, on_line], axis=1).reshape(-1)
    place = jnp.concatenate(
        [jnp.stack([slab]), where_green, jnp.stack([1 - c])]
    ).astype(jnp.int32)
    sources = 4 * sources_here

    def touch(array):
        return array[:8, :128]

    r1_a = send(own, moves[0])
    r2_a = send(r1_a, moves[1])
    r1_b = send(after(crossed, r1_a), moves[0])
    r3_a = send(r2_a, moves[2])
    r2_b = send(after(r1_b, touch(r2_a)), moves[1])
    res_1 = residual(place, (r1_a, after(r1_b, r2_a)), sources)
    r4_a = send(after(r3_a, res_1), moves[3])
    r3_b = send(after(r2_b, touch(r3_a)), moves[2])
    res_2 = residual(place, (r2_a, after(r2_b, r3_a)), sources)
    begun = begin(place, (r4_a, own), sources)
    r4_b = send(after(r3_b, res_2), moves[4])

    field_core = send(after(source_fields, r1_a), to_core)
    field_x = send(after(source_fields, crossed_here), to_x)
    field_far = send(after(field_x, res_1), to_core)
    fields = (source_fields, field_core, field_x, field_far)

    blocks = green_fields.reshape(2, 2, 2, -1, green_fields.shape[2])
    near, away_green = halves(place_x, after(blocks, r1_a))
    far = send(after(away_green, r2_b), to_x)

    res_3 = residual(place, (r3_a, r3_b), sources)
    early = correlated((res_1, res_2), fields)
    middle = correlated((after(res_3, early),), fields)
    far_core = send(after(far, middle, begun), to_core)
    greens = (near, send(near, to_core), far, far_core)
    folded = fold(place, (early, middle), greens)
    partial = last(place, (r4_b, crossed), begun, folded, greens, fields)[0]
    here = partial + send(partial, to_core)
    there = send(partial, to_x) + send(partial, to_both)
    return here + there


def gathered(trace_values, trace_owner, trace_source, source_fields, green_fields):
    values = trace_values[0]
    half_width = values.shape[1] // 2
    src_count = lax.axis_size("src")
    sources_here = source_fields.shape[1]
    slab_index = lax.axis_index("slab")
    high = trace_owner[0, :, 0] * (sources_here // 32) + trace_source[0] // 32
    low = trace_source[0] % 32
    per_slab = sources_here // 32
    piece_values = lax.all_gather(values, "slab", axis=0, tiled=True)
    owners = trace_owner[0, :, 0].astype(jnp.bfloat16)
    high_part = (trace_source[0] // 32).astype(jnp.bfloat16)
    low_part = low.astype(jnp.bfloat16)
    piece_ids = lax.all_gather(
        jnp.stack([owners, high_part, low_part]), "slab", axis=1, tiled=True
    )
    ids = jnp.arange(sources_here, dtype=jnp.int32)
    picks = (
        ((ids // 32).astype(jnp.bfloat16)[:, None] == piece_ids[1][None, :])
        & ((ids % 32).astype(jnp.bfloat16)[:, None] == piece_ids[2][None, :])
        & (piece_ids[0][None, :] == slab_index.astype(jnp.bfloat16))
    )
    assembled = jnp.dot(
        picks.astype(jnp.bfloat16), piece_values, preferred_element_type=jnp.float32
    )
    rows = lax.all_gather(assembled.astype(jnp.bfloat16), "src", axis=1, tiled=True)
    split_rows = rows.reshape(sources_here, src_count, 2, half_width)
    res_real = split_rows[:, :, 0, :].reshape(sources_here, src_count * half_width)
    res_imag = split_rows[:, :, 1, :].reshape(sources_here, src_count * half_width)
    green = lax.all_gather(green_fields, "slab", axis=1, tiled=True)
    dot = functools.partial(jnp.dot, preferred_element_type=jnp.float32)
    adj_real = dot(res_real, green[0]) + dot(res_imag, green[1])
    adj_imag = dot(res_real, green[1]) - dot(res_imag, green[0])
    partial = jnp.sum(
        source_fields[0].astype(jnp.float32) * adj_real
        - source_fields[1].astype(jnp.float32) * adj_imag,
        axis=0,
    )
    return lax.psum(partial, "slab")


def solution(mesh):
    in_specs = (
        P("src", "slab", None),
        P("src", "slab", None),
        P("src", "slab"),
        P(None, "slab", "src"),
        P(None, "slab", "src"),
    )
    n_slab, n_src = mesh.shape["slab"], mesh.shape["src"]
    if n_slab == 2 * 2 and n_src == 2 * 4:
        on_device = functools.partial(paired, n_src)
    else:
        on_device = gathered
    return jax.shard_map(
        on_device, mesh=mesh, in_specs=in_specs, out_specs=P("src"), check_vma=False
    )
```

```python
import functools

import jax
import jax.numpy as jnp
import numpy as np
from jax import lax
from jax.experimental import pallas as pl
from jax.experimental.pallas import tpu as pltpu
from jax.sharding import PartitionSpec as P

AXES = ("slab", "src")
PAD = 16
TILE = 256
VMEM_LIMIT = 24 * 1024 * 1024


def params():
    return pltpu.CompilerParams(vmem_limit_bytes=VMEM_LIMIT)


def light(name):
    return pl.CostEstimate(
        flops=COSTS.get(name, 1000), bytes_accessed=1000, transcendentals=0
    )


SMEM_SPEC = pl.BlockSpec(memory_space=pltpu.SMEM)
VMEM_SPEC = pl.BlockSpec(memory_space=pltpu.VMEM)


COSTS = {}
ORDER = {'r1_b': ('r1_a',), 'r4_a': ('res_1',), 'r4_b': ('res_2',), 'res_1': ('r2_a',), 'res_2': ('r3_a',), 'field_core': ('r1_a',), 'field_x': ('crossed_here',), 'field_far': ('res_1',), 'halves': ('r1_a',), 'far': ('r3_a',), 'res_3': ('early',), 'far_core': ('res_3',), }


def number(x, c, y, z, n_src):
    return (2 * x + c) * n_src + 2 * z + y


def receivers(values, first, rows, out_ref, spot):
    quarter = values.shape[1] // 4
    for part in range(2):
        low = values[:, 2 * part * quarter : (2 * part + 1) * quarter]
        high = values[:, (2 * part + 1) * quarter : (2 * part + 2) * quarter]
        lanes = pl.ds(part * quarter, quarter)
        out_ref[pl.ds(spot, rows), lanes] = jnp.where(first, low, high)


def id_rows(trace_owner, trace_source, sources_here):
    ids = trace_source[0]
    high = trace_owner[0, :, 0] * (sources_here // TILE) + ids // TILE
    rows = jnp.stack([high, ids % TILE])
    return jnp.pad(rows, ((0, PAD - 2), (0, 0))).astype(jnp.bfloat16)


def cut_kernel(place, values, ids, near_ref, away_ref):
    rows = values.shape[0]
    first = place[0] == 0
    receivers(values, first, rows, near_ref, 0)
    receivers(values, jnp.logical_not(first), rows, away_ref, 0)
    tiles = rows // TILE
    block = jnp.concatenate(
        [
            ids[kind : kind + 1, j * TILE : (j + 1) * TILE]
            for kind in range(2)
            for j in range(tiles)
        ]
        + [jnp.zeros((PAD - 2 * tiles, TILE), jnp.bfloat16)],
        axis=0,
    )
    near_ref[rows:, :] = block
    away_ref[rows:, :] = block


def cut(place, values, ids):
    rows, width = values.shape
    shape = jax.ShapeDtypeStruct((rows + PAD, width // 2), jnp.bfloat16)
    return pl.pallas_call(
        cut_kernel,
        name="cut",
        out_shape=(shape, shape),
        in_specs=[SMEM_SPEC] + [VMEM_SPEC] * 2,
        out_specs=(VMEM_SPEC, VMEM_SPEC),
        compiler_params=params(),
        cost_estimate=light("cut"),
    )(place, values, ids)


def join_kernel(mine, other, out_ref):
    rows = mine.shape[0] - PAD
    tiles = rows // TILE
    out_ref[:rows, :] = mine[:rows, :]
    out_ref[rows : 2 * rows, :] = other[:rows, :]
    ids = [mine[rows:, :], other[rows:, :]]
    pieces = [part[kind * tiles : (kind + 1) * tiles] for kind in range(2) for part in ids]
    pad = jnp.zeros((PAD - 4 * tiles, TILE), jnp.bfloat16)
    out_ref[2 * rows :, :] = jnp.concatenate(pieces + [pad], axis=0)


def join(mine, other):
    rows, width = mine.shape
    return pl.pallas_call(
        join_kernel,
        name="join",
        out_shape=jax.ShapeDtypeStruct((2 * rows - PAD, width), jnp.bfloat16),
        in_specs=[VMEM_SPEC] * 2,
        out_specs=VMEM_SPEC,
        compiler_params=params(),
        cost_estimate=light("join"),
    )(mine, other)


def halves_kernel(place, blocks, near_ref, away_ref):
    first = place[0] == 0
    for p in range(blocks.shape[0]):
        for line in range(blocks.shape[1]):
            low, high = blocks[p, line, 0], blocks[p, line, 1]
            near_ref[p, line] = jnp.where(first, low, high)
            away_ref[p, line] = jnp.where(first, high, low)


def halves(place, blocks):
    shape = jax.ShapeDtypeStruct(blocks.shape[:2] + blocks.shape[3:], blocks.dtype)
    return pl.pallas_call(
        halves_kernel,
        name="halves",
        out_shape=(shape, shape),
        in_specs=[SMEM_SPEC, VMEM_SPEC],
        out_specs=(VMEM_SPEC, VMEM_SPEC),
        compiler_params=params(),
        cost_estimate=light("halves"),
    )(place, blocks)


def fetch(which, candidates, target, sem):
    for k, ref in enumerate(candidates):

        @pl.when(which == k)
        def _(ref=ref):
            copy = pltpu.make_async_copy(ref, target, sem)
            copy.start()
            copy.wait()


def assemble(slab, pieces, group, start=None):
    traces = pieces[0].shape[0] - PAD
    tiles = traces // TILE
    iota = lax.broadcasted_iota(jnp.int32, (TILE, TILE), 0).astype(jnp.bfloat16)
    out = []
    owner = slab ^ group
    per = 2
    for h in range(per):
        name = (owner * per + h).astype(jnp.float32).astype(jnp.bfloat16)
        total = None if start is None else start[h * TILE : (h + 1) * TILE, :]
        for piece in pieces:
            masks = []
            for j in range(tiles):
                high = piece[traces + j : traces + j + 1, :]
                low = piece[traces + tiles + j : traces + tiles + j + 1, :]
                wanted = jnp.where(high == name, low, jnp.bfloat16(-1.0))
                masks.append(
                    jnp.where(iota == wanted, jnp.bfloat16(1.0), jnp.bfloat16(0.0))
                )
            mask = jnp.concatenate(masks, axis=1)
            term = jnp.dot(
                mask, piece[:traces, :], preferred_element_type=jnp.float32
            )
            total = term if total is None else total + term
        out.append(total)
    return jnp.concatenate(out, axis=0)


def residual_kernel(n, place, *refs):
    out_ref = refs[n]
    rows = out_ref.shape[0] // 4
    for group in range(4):
        out_ref[group * rows : (group + 1) * rows, :] = assemble(
            place[0], refs[:n], group
        ).astype(out_ref.dtype)


def residual(place, pieces, sources):
    return pl.pallas_call(
        functools.partial(residual_kernel, len(pieces)),
        name="residual",
        out_shape=jax.ShapeDtypeStruct((sources, pieces[0].shape[1]), jnp.bfloat16),
        in_specs=[SMEM_SPEC] + [VMEM_SPEC] * len(pieces),
        out_specs=VMEM_SPEC,
        compiler_params=params(),
        cost_estimate=light("residual"),
    )(place, *pieces)


def begin_kernel(n, place, *refs):
    cand, (out_ref, piece, sem) = refs[:n], refs[n:]
    fetch(place[9], cand, piece, sem)
    rows = out_ref.shape[0] // 4
    for group in range(4):
        out_ref[group * rows : (group + 1) * rows, :] = assemble(
            place[0], (piece,), group
        )


def begin(place, cand, sources):
    shape = cand[0].shape
    return pl.pallas_call(
        functools.partial(begin_kernel, len(cand)),
        name="begin",
        out_shape=jax.ShapeDtypeStruct((sources, shape[1]), jnp.float32),
        in_specs=[SMEM_SPEC] + [VMEM_SPEC] * len(cand),
        out_specs=VMEM_SPEC,
        scratch_shapes=[pltpu.VMEM(shape, jnp.bfloat16), pltpu.SemaphoreType.DMA],
        compiler_params=params(),
        cost_estimate=light("begin"),
    )(place, *cand)


def correlate(res, fields):
    contract = (((0,), (0,)), ((), ()))
    dot = functools.partial(
        lax.dot_general,
        dimension_numbers=contract,
        preferred_element_type=jnp.float32,
    )
    half = res[0].shape[1] // 2
    real, imag = None, None
    for piece, field in zip(res, fields):
        with_real, with_imag = dot(piece, field[0]), dot(piece, field[1])
        first = with_real[:half] + with_imag[half:]
        second = with_real[half:] - with_imag[:half]
        real = first if real is None else real + first
        imag = second if imag is None else imag + second
    return real, imag


def correlate_kernel(n_res, *refs):
    res, out_ref = refs[:n_res], refs[-1]
    fields = refs[n_res:-1]
    rows = res[0].shape[0] // 4
    for k, ref in enumerate(res):
        parts = [ref[g * rows : (g + 1) * rows, :] for g in range(4)]
        real, imag = correlate(parts, fields)
        out_ref[k, 0] = real
        out_ref[k, 1] = imag


def correlated(res, fields):
    half, cells = res[0].shape[1] // 2, fields[0].shape[2]
    return pl.pallas_call(
        functools.partial(correlate_kernel, len(res)),
        name="correlate",
        out_shape=jax.ShapeDtypeStruct((len(res), 2, half, cells), jnp.float32),
        in_specs=[VMEM_SPEC] * (len(res) + len(fields)),
        out_specs=VMEM_SPEC,
        compiler_params=params(),
        cost_estimate=light("correlate"),
    )(*res, *fields)


def fetch_green(place, slot, greens, target, sems):
    group, line = place[1 + 2 * slot], place[2 + 2 * slot]
    for j, ref in enumerate(greens):

        @pl.when(group == j)
        def _(ref=ref):
            for p in range(2):
                pltpu.make_async_copy(ref.at[p, line], target.at[p], sems.at[p]).start()

    def wait():
        for p in range(2):
            pltpu.make_async_copy(greens[0].at[p, 0], target.at[p], sems.at[p]).wait()

    return wait


def fold_kernel(n, place, *refs):
    factors, greens, (out_ref, green, sems) = refs[:n], refs[n : n + 4], refs[n + 4 :]
    slots = [(ref, k) for ref in factors for k in range(ref.shape[0])]
    waits = [
        fetch_green(place, j, greens, green.at[j], sems.at[j])
        for j in range(len(slots))
    ]
    total = None
    for j, (ref, k) in enumerate(slots):
        waits[j]()
        for p in range(2):
            term = green[j, p].astype(jnp.float32) * ref[k, p]
            total = term if total is None else total + term
    out_ref[...] = jnp.sum(total, axis=0, keepdims=True)


def fold(place, factors, greens):
    slots = sum(f.shape[0] for f in factors)
    return pl.pallas_call(
        functools.partial(fold_kernel, len(factors)),
        name="fold",
        out_shape=jax.ShapeDtypeStruct((1, factors[0].shape[3]), jnp.float32),
        in_specs=[SMEM_SPEC] + [VMEM_SPEC] * (len(factors) + len(greens)),
        out_specs=VMEM_SPEC,
        scratch_shapes=[
            pltpu.VMEM((slots, 2) + greens[0].shape[2:], jnp.bfloat16),
            pltpu.SemaphoreType.DMA((slots, 2)),
        ],
        compiler_params=params(),
        cost_estimate=light("fold"),
    )(place, *factors, *greens)


def last_kernel(n_b, place, *refs):
    cand_b, (begun, folded) = refs[:n_b], refs[n_b : n_b + 2]
    greens, fields = refs[n_b + 2 : n_b + 6], refs[n_b + 6 : n_b + 10]
    out_ref, piece, green, sem, sems = refs[n_b + 10 :]
    wait = fetch_green(place, 3, greens, green, sems)
    fetch(place[9], cand_b, piece, sem)
    rows = begun.shape[0] // 4
    parts = [
        assemble(
            place[0], (piece,), g, begun[g * rows : (g + 1) * rows, :]
        ).astype(jnp.bfloat16)
        for g in range(4)
    ]
    real, imag = correlate(parts, fields)
    wait()
    total = green[0].astype(jnp.float32) * real + green[1].astype(jnp.float32) * imag
    out_ref[...] = folded[...] + jnp.sum(total, axis=0, keepdims=True)


def last(place, cand_b, begun, folded, greens, fields):
    return pl.pallas_call(
        functools.partial(last_kernel, len(cand_b)),
        name="last",
        out_shape=jax.ShapeDtypeStruct(folded.shape, jnp.float32),
        in_specs=[SMEM_SPEC]
        + [VMEM_SPEC] * (len(cand_b) + 2 + len(greens) + len(fields)),
        out_specs=VMEM_SPEC,
        scratch_shapes=[
            pltpu.VMEM(cand_b[0].shape, jnp.bfloat16),
            pltpu.VMEM((2,) + greens[0].shape[2:], jnp.bfloat16),
            pltpu.SemaphoreType.DMA,
            pltpu.SemaphoreType.DMA((2,)),
        ],
        compiler_params=params(),
        cost_estimate=light("last"),
    )(place, *cand_b, begun, folded, *greens, *fields)


def paired(n_src, trace_values, trace_owner, trace_source, source_fields, green_fields):
    values = trace_values[0]
    sources_here = source_fields.shape[1]
    slab = lax.axis_index("slab")
    src = lax.axis_index("src")
    x, c = slab // 2, slab % 2
    z, y = src // 2, src % 2
    lines = range(n_src // 2)

    def send(array, moves):
        pairs = [
            (number(*a, n_src), number(*b, n_src)) for a, b in moves
        ]
        return lax.ppermute(array, AXES, pairs)

    everywhere = [
        (a, b, d, e) for a in range(2) for b in range(2) for d in range(2) for e in lines
    ]
    to_core = [((a, b, d, e), (a, 1 - b, d, e)) for a, b, d, e in everywhere]
    to_x = [((a, b, d, e), (1 - a, b, d, e)) for a, b, d, e in everywhere]
    to_both = [((a, b, d, e), (1 - a, 1 - b, d, e)) for a, b, d, e in everywhere]

    def after(array, *earlier):
        return lax.optimization_barrier((array, *earlier))[0]

    place_x = jnp.stack([x]).astype(jnp.int32)
    ids = id_rows(trace_owner, trace_source, sources_here)
    kept, away = cut(place_x, values, ids)
    kept_core = send(kept, to_core)
    own = join(kept, kept_core)
    crossed_here = after(send(away, to_x), own)
    crossed = join(crossed_here, send(crossed_here, to_core))

    moves = []
    for steps in (
        [(0, 0, 1, None), (1, 0, 1, 1), (0, 1, 0, 0), (1, 1, 0, 2)],
        [(0, 0, 1, None), (1, 0, 0, 1), (0, 1, 0, 0), (1, 1, 1, 2)],
        [(0, 0, 1, None), (1, 0, 1, 1), (0, 1, 0, 2), (1, 1, 0, 0)],
        [(0, 0, 1, None), (1, 1, 1, 2)],
        [(1, 0, 1, 1), (0, 1, 1, 0)],
    ):
        pairs = []
        for here_c, here_z, there_c, there_z in steps:
            for a in range(2):
                for d in range(2):
                    for e in (here_z, len(lines) - 1 - here_z):
                        if there_z is None:
                            target = (a, there_c, 1 - d, e)
                        else:
                            far_z = there_z if e == here_z else len(lines) - 1 - there_z
                            target = (a, there_c, d, far_z)
                        pairs.append(((a, here_c, d, e), target))
        moves.append(pairs)
    brought = np.array(
        [
            [[(1, 0), (2, 0), (3, 0), (0, 0)], [(0, 1), (1, 1), (2, 1), (3, 1)]],
            [[(2, 0), (0, 1), (3, 1), (1, 0)], [(0, 0), (3, 0), (1, 1), (2, 1)]],
        ],
        np.int32,
    )
    mirrored = brought[::-1].copy()
    mirrored[..., 0] = len(lines) - 1 - mirrored[..., 0]
    table = jnp.asarray(np.concatenate([brought, mirrored]))

    mine_now = lax.dynamic_index_in_dim(
        lax.dynamic_index_in_dim(table, z, 0, keepdims=False), c, 0, keepdims=False
    )
    groups = jnp.bitwise_xor(mine_now[:, 0], slab)
    on_line = jnp.bitwise_xor(mine_now[:, 1], y)
    where_green = jnp.stack([groups, on_line], axis=1).reshape(-1)
    place = jnp.concatenate(
        [jnp.stack([slab]), where_green, jnp.stack([1 - c])]
    ).astype(jnp.int32)
    sources = 4 * sources_here

    blocks = green_fields.reshape(2, 2, 2, -1, green_fields.shape[2])
    made = {"own": own, "crossed": crossed, "crossed_here": crossed_here}
    steps = {}

    def get(name):
        if name not in made:
            made[name] = None
            made[name] = steps[name]()
        return made[name]

    def behind(name, array):
        return after(array, *[get(k) for k in ORDER.get(name, ())])

    steps["r1_a"] = lambda: send(own, moves[0])
    steps["r2_a"] = lambda: send(behind("r2_a", get("r1_a")), moves[1])
    steps["r3_a"] = lambda: send(behind("r3_a", get("r2_a")), moves[2])
    steps["r4_a"] = lambda: send(behind("r4_a", get("r3_a")), moves[3])
    steps["r1_b"] = lambda: send(behind("r1_b", crossed), moves[0])
    steps["r2_b"] = lambda: send(behind("r2_b", get("r1_b")), moves[1])
    steps["r3_b"] = lambda: send(behind("r3_b", get("r2_b")), moves[2])
    steps["r4_b"] = lambda: send(behind("r4_b", get("r3_b")), moves[4])
    steps["res_1"] = lambda: residual(
        place, (get("r1_a"), behind("res_1", get("r1_b"))), sources
    )
    steps["res_2"] = lambda: residual(
        place, (get("r2_a"), behind("res_2", get("r2_b"))), sources
    )
    steps["res_3"] = lambda: residual(
        place, (get("r3_a"), behind("res_3", get("r3_b"))), sources
    )
    steps["begun"] = lambda: begin(place, (behind("begun", get("r4_a")), own), sources)
    steps["field_core"] = lambda: send(behind("field_core", source_fields), to_core)
    steps["field_x"] = lambda: send(behind("field_x", source_fields), to_x)
    steps["field_far"] = lambda: send(behind("field_far", get("field_x")), to_core)
    steps["halves"] = lambda: halves(place_x, behind("halves", blocks))
    steps["near"] = lambda: get("halves")[0]
    steps["away"] = lambda: get("halves")[1]
    steps["near_core"] = lambda: send(behind("near_core", get("near")), to_core)
    steps["far"] = lambda: send(behind("far", get("away")), to_x)
    steps["far_core"] = lambda: send(behind("far_core", get("far")), to_core)
    steps["fields"] = lambda: (
        source_fields, get("field_core"), get("field_x"), get("field_far")
    )
    steps["early"] = lambda: correlated(
        (get("res_1"), behind("early", get("res_2"))), get("fields")
    )
    steps["middle"] = lambda: correlated(
        (behind("middle", get("res_3")),), get("fields")
    )
    greens = [get(k) for k in ("near", "near_core", "far", "far_core")]
    folded = fold(
        place, (get("early"), behind("fold", get("middle"))), greens
    )
    partial = last(
        place, (get("r4_b"), crossed), get("begun"), folded, greens, get("fields")
    )[0]
    here = partial + send(partial, to_core)
    there = send(partial, to_x) + send(partial, to_both)
    return here + there


def gathered(trace_values, trace_owner, trace_source, source_fields, green_fields):
    values = trace_values[0]
    half_width = values.shape[1] // 2
    src_count = lax.axis_size("src")
    sources_here = source_fields.shape[1]
    slab_index = lax.axis_index("slab")
    high = trace_owner[0, :, 0] * (sources_here // 32) + trace_source[0] // 32
    low = trace_source[0] % 32
    per_slab = sources_here // 32
    piece_values = lax.all_gather(values, "slab", axis=0, tiled=True)
    owners = trace_owner[0, :, 0].astype(jnp.bfloat16)
    high_part = (trace_source[0] // 32).astype(jnp.bfloat16)
    low_part = low.astype(jnp.bfloat16)
    piece_ids = lax.all_gather(
        jnp.stack([owners, high_part, low_part]), "slab", axis=1, tiled=True
    )
    ids = jnp.arange(sources_here, dtype=jnp.int32)
    picks = (
        ((ids // 32).astype(jnp.bfloat16)[:, None] == piece_ids[1][None, :])
        & ((ids % 32).astype(jnp.bfloat16)[:, None] == piece_ids[2][None, :])
        & (piece_ids[0][None, :] == slab_index.astype(jnp.bfloat16))
    )
    assembled = jnp.dot(
        picks.astype(jnp.bfloat16), piece_values, preferred_element_type=jnp.float32
    )
    rows = lax.all_gather(assembled.astype(jnp.bfloat16), "src", axis=1, tiled=True)
    split_rows = rows.reshape(sources_here, src_count, 2, half_width)
    res_real = split_rows[:, :, 0, :].reshape(sources_here, src_count * half_width)
    res_imag = split_rows[:, :, 1, :].reshape(sources_here, src_count * half_width)
    green = lax.all_gather(green_fields, "slab", axis=1, tiled=True)
    dot = functools.partial(jnp.dot, preferred_element_type=jnp.float32)
    adj_real = dot(res_real, green[0]) + dot(res_imag, green[1])
    adj_imag = dot(res_real, green[1]) - dot(res_imag, green[0])
    partial = jnp.sum(
        source_fields[0].astype(jnp.float32) * adj_real
        - source_fields[1].astype(jnp.float32) * adj_imag,
        axis=0,
    )
    return lax.psum(partial, "slab")


def solution(mesh):
    in_specs = (
        P("src", "slab", None),
        P("src", "slab", None),
        P("src", "slab"),
        P(None, "slab", "src"),
        P(None, "slab", "src"),
    )
    n_slab, n_src = mesh.shape["slab"], mesh.shape["src"]
    if n_slab == 2 * 2 and n_src == 2 * 4:
        on_device = functools.partial(paired, n_src)
    else:
        on_device = gathered
    return jax.shard_map(
        on_device, mesh=mesh, in_specs=in_specs, out_specs=P("src"), check_vma=False
    )
```

```python
import functools

import jax
import jax.numpy as jnp
import numpy as np
from jax import lax
from jax.experimental import pallas as pl
from jax.experimental.pallas import tpu as pltpu
from jax.sharding import PartitionSpec as P

AXES = ("slab", "src")
PAD = 16
TILE = 256
VMEM_LIMIT = 24 * 1024 * 1024


def params():
    return pltpu.CompilerParams(vmem_limit_bytes=VMEM_LIMIT)


def light():
    return pl.CostEstimate(flops=1000, bytes_accessed=1000, transcendentals=0)


SMEM_SPEC = pl.BlockSpec(memory_space=pltpu.SMEM)
VMEM_SPEC = pl.BlockSpec(memory_space=pltpu.VMEM)


ORDER = {
    "r4_a": ("res_1",),
    "r4_b": ("res_2",),
    "res_1": ("r2_a",),
    "res_2": ("r3_a",),
    "field_core": ("r1_a",),
    "field_x": ("own",),
    "field_far": ("res_1",),
    "halves": ("r1_a",),
    "far": ("r3_a", "near_core",),
    "res_3": ("early",),
    "far_core": ("res_3",),
    "near_core": ("r2_a",),
}


def number(x, c, y, z, n_src):
    return (2 * x + c) * n_src + 2 * z + y


def receivers(values, first, rows, out_ref, spot):
    quarter = values.shape[1] // 4
    for part in range(2):
        low = values[:, 2 * part * quarter : (2 * part + 1) * quarter]
        high = values[:, (2 * part + 1) * quarter : (2 * part + 2) * quarter]
        lanes = pl.ds(part * quarter, quarter)
        out_ref[pl.ds(spot, rows), lanes] = jnp.where(first, low, high)


def id_rows(trace_owner, trace_source, sources_here):
    ids = trace_source[0]
    high = trace_owner[0, :, 0] * (sources_here // TILE) + ids // TILE
    rows = jnp.stack([high, ids % TILE])
    return jnp.pad(rows, ((0, PAD - 2), (0, 0))).astype(jnp.bfloat16)


def cut_kernel(place, values, ids, near_ref, away_ref):
    rows = values.shape[0]
    first = place[0] == 0
    receivers(values, first, rows, near_ref, 0)
    receivers(values, jnp.logical_not(first), rows, away_ref, 0)
    tiles = rows // TILE
    block = jnp.concatenate(
        [
            ids[kind : kind + 1, j * TILE : (j + 1) * TILE]
            for kind in range(2)
            for j in range(tiles)
        ]
        + [jnp.zeros((PAD - 2 * tiles, TILE), jnp.bfloat16)],
        axis=0,
    )
    near_ref[rows:, :] = block
    away_ref[rows:, :] = block


def cut(place, values, ids):
    rows, width = values.shape
    shape = jax.ShapeDtypeStruct((rows + PAD, width // 2), jnp.bfloat16)
    return pl.pallas_call(
        cut_kernel,
        name="cut",
        out_shape=(shape, shape),
        in_specs=[SMEM_SPEC] + [VMEM_SPEC] * 2,
        out_specs=(VMEM_SPEC, VMEM_SPEC),
        compiler_params=params(),
        cost_estimate=light(),
    )(place, values, ids)


def join_kernel(mine, other, out_ref):
    rows = mine.shape[0] - PAD
    tiles = rows // TILE
    out_ref[:rows, :] = mine[:rows, :]
    out_ref[rows : 2 * rows, :] = other[:rows, :]
    ids = [mine[rows:, :], other[rows:, :]]
    pieces = [part[kind * tiles : (kind + 1) * tiles] for kind in range(2) for part in ids]
    pad = jnp.zeros((PAD - 4 * tiles, TILE), jnp.bfloat16)
    out_ref[2 * rows :, :] = jnp.concatenate(pieces + [pad], axis=0)


def join(mine, other):
    rows, width = mine.shape
    return pl.pallas_call(
        join_kernel,
        name="join",
        out_shape=jax.ShapeDtypeStruct((2 * rows - PAD, width), jnp.bfloat16),
        in_specs=[VMEM_SPEC] * 2,
        out_specs=VMEM_SPEC,
        compiler_params=params(),
        cost_estimate=light(),
    )(mine, other)


def halves_kernel(place, blocks, near_ref, away_ref):
    first = place[0] == 0
    for p in range(blocks.shape[0]):
        for line in range(blocks.shape[1]):
            low, high = blocks[p, line, 0], blocks[p, line, 1]
            near_ref[p, line] = jnp.where(first, low, high)
            away_ref[p, line] = jnp.where(first, high, low)


def halves(place, blocks):
    shape = jax.ShapeDtypeStruct(blocks.shape[:2] + blocks.shape[3:], blocks.dtype)
    return pl.pallas_call(
        halves_kernel,
        name="halves",
        out_shape=(shape, shape),
        in_specs=[SMEM_SPEC, VMEM_SPEC],
        out_specs=(VMEM_SPEC, VMEM_SPEC),
        compiler_params=params(),
        cost_estimate=light(),
    )(place, blocks)


def choose(which, candidates, target):
    first, second = candidates
    target[...] = jnp.where(which == 0, first[...], second[...])


def assemble(slab, pieces, group, per, start=None):
    traces = pieces[0].shape[0] - PAD
    tiles = traces // TILE
    iota = lax.broadcasted_iota(jnp.int32, (TILE, TILE), 0).astype(jnp.bfloat16)
    out = []
    owner = slab ^ group
    for h in range(per):
        name = (owner * per + h).astype(jnp.float32).astype(jnp.bfloat16)
        total = None if start is None else start[h * TILE : (h + 1) * TILE, :]
        for piece in pieces:
            masks = []
            for j in range(tiles):
                high = piece[traces + j : traces + j + 1, :]
                low = piece[traces + tiles + j : traces + tiles + j + 1, :]
                wanted = jnp.where(high == name, low, jnp.bfloat16(-1.0))
                masks.append(
                    jnp.where(iota == wanted, jnp.bfloat16(1.0), jnp.bfloat16(0.0))
                )
            mask = jnp.concatenate(masks, axis=1)
            term = jnp.dot(
                mask, piece[:traces, :], preferred_element_type=jnp.float32
            )
            total = term if total is None else total + term
        out.append(total)
    return jnp.concatenate(out, axis=0)


def residual_kernel(n, place, *refs):
    out_ref = refs[n]
    rows = out_ref.shape[0] // 4
    for group in range(4):
        out_ref[group * rows : (group + 1) * rows, :] = assemble(
            place[0], refs[:n], group, rows // TILE
        ).astype(out_ref.dtype)


def residual(place, pieces, sources):
    return pl.pallas_call(
        functools.partial(residual_kernel, len(pieces)),
        name="residual",
        out_shape=jax.ShapeDtypeStruct((sources, pieces[0].shape[1]), jnp.bfloat16),
        in_specs=[SMEM_SPEC] + [VMEM_SPEC] * len(pieces),
        out_specs=VMEM_SPEC,
        compiler_params=params(),
        cost_estimate=light(),
    )(place, *pieces)


def begin_kernel(n, place, *refs):
    cand, (out_ref, piece) = refs[:n], refs[n:]
    choose(place[9], cand, piece)
    rows = out_ref.shape[0] // 4
    for group in range(4):
        out_ref[group * rows : (group + 1) * rows, :] = assemble(
            place[0], (piece,), group, rows // TILE
        )


def begin(place, cand, sources):
    shape = cand[0].shape
    return pl.pallas_call(
        functools.partial(begin_kernel, len(cand)),
        name="begin",
        out_shape=jax.ShapeDtypeStruct((sources, shape[1]), jnp.float32),
        in_specs=[SMEM_SPEC] + [VMEM_SPEC] * len(cand),
        out_specs=VMEM_SPEC,
        scratch_shapes=[pltpu.VMEM(shape, jnp.bfloat16)],
        compiler_params=params(),
        cost_estimate=light(),
    )(place, *cand)


def correlate(res, fields):
    contract = (((0,), (0,)), ((), ()))
    dot = functools.partial(
        lax.dot_general,
        dimension_numbers=contract,
        preferred_element_type=jnp.float32,
    )
    half = res[0].shape[1] // 2
    real, imag = None, None
    for piece, field in zip(res, fields):
        with_real, with_imag = dot(piece, field[0]), dot(piece, field[1])
        first = with_real[:half] + with_imag[half:]
        second = with_real[half:] - with_imag[:half]
        real = first if real is None else real + first
        imag = second if imag is None else imag + second
    return real, imag


def correlate_kernel(n_res, *refs):
    res, out_ref = refs[:n_res], refs[-1]
    fields = refs[n_res:-1]
    rows = res[0].shape[0] // 4
    for k, ref in enumerate(res):
        parts = [ref[g * rows : (g + 1) * rows, :] for g in range(4)]
        real, imag = correlate(parts, fields)
        out_ref[k, 0] = real
        out_ref[k, 1] = imag


def correlated(res, fields):
    half, cells = res[0].shape[1] // 2, fields[0].shape[2]
    return pl.pallas_call(
        functools.partial(correlate_kernel, len(res)),
        name="correlate",
        out_shape=jax.ShapeDtypeStruct((len(res), 2, half, cells), jnp.float32),
        in_specs=[VMEM_SPEC] * (len(res) + len(fields)),
        out_specs=VMEM_SPEC,
        compiler_params=params(),
        cost_estimate=light(),
    )(*res, *fields)


def fetch_green(place, slot, greens, target, sems):
    group, line = place[1 + 2 * slot], place[2 + 2 * slot]
    for j, ref in enumerate(greens):

        @pl.when(group == j)
        def _(ref=ref):
            for p in range(2):
                pltpu.make_async_copy(ref.at[p, line], target.at[p], sems.at[p]).start()

    def wait():
        for p in range(2):
            pltpu.make_async_copy(greens[0].at[p, 0], target.at[p], sems.at[p]).wait()

    return wait


def fold_kernel(n, place, *refs):
    factors, greens, (out_ref, green, sems) = refs[:n], refs[n : n + 4], refs[n + 4 :]
    slots = [(ref, k) for ref in factors for k in range(ref.shape[0])]
    waits = [
        fetch_green(place, j, greens, green.at[j], sems.at[j])
        for j in range(len(slots))
    ]
    total = None
    for j, (ref, k) in enumerate(slots):
        waits[j]()
        for p in range(2):
            term = green[j, p].astype(jnp.float32) * ref[k, p]
            total = term if total is None else total + term
    out_ref[...] = jnp.sum(total, axis=0, keepdims=True)


def fold(place, factors, greens):
    slots = sum(f.shape[0] for f in factors)
    return pl.pallas_call(
        functools.partial(fold_kernel, len(factors)),
        name="fold",
        out_shape=jax.ShapeDtypeStruct((1, factors[0].shape[3]), jnp.float32),
        in_specs=[SMEM_SPEC] + [VMEM_SPEC] * (len(factors) + len(greens)),
        out_specs=VMEM_SPEC,
        scratch_shapes=[
            pltpu.VMEM((slots, 2) + greens[0].shape[2:], jnp.bfloat16),
            pltpu.SemaphoreType.DMA((slots, 2)),
        ],
        compiler_params=params(),
        cost_estimate=light(),
    )(place, *factors, *greens)


def last_kernel(n_b, place, *refs):
    cand_b, (begun, folded) = refs[:n_b], refs[n_b : n_b + 2]
    greens, fields = refs[n_b + 2 : n_b + 6], refs[n_b + 6 : n_b + 10]
    out_ref, piece, green, sems = refs[n_b + 10 :]
    wait = fetch_green(place, 3, greens, green, sems)
    choose(place[9], cand_b, piece)
    rows = begun.shape[0] // 4
    parts = [
        assemble(
            place[0],
            (piece,),
            g,
            rows // TILE,
            begun[g * rows : (g + 1) * rows, :],
        ).astype(jnp.bfloat16)
        for g in range(4)
    ]
    real, imag = correlate(parts, fields)
    wait()
    total = green[0].astype(jnp.float32) * real + green[1].astype(jnp.float32) * imag
    out_ref[...] = folded[...] + jnp.sum(total, axis=0, keepdims=True)


def last(place, cand_b, begun, folded, greens, fields):
    return pl.pallas_call(
        functools.partial(last_kernel, len(cand_b)),
        name="last",
        out_shape=jax.ShapeDtypeStruct(folded.shape, jnp.float32),
        in_specs=[SMEM_SPEC]
        + [VMEM_SPEC] * (len(cand_b) + 2 + len(greens) + len(fields)),
        out_specs=VMEM_SPEC,
        scratch_shapes=[
            pltpu.VMEM(cand_b[0].shape, jnp.bfloat16),
            pltpu.VMEM((2,) + greens[0].shape[2:], jnp.bfloat16),
            pltpu.SemaphoreType.DMA((2,)),
        ],
        compiler_params=params(),
        cost_estimate=light(),
    )(place, *cand_b, begun, folded, *greens, *fields)


def paired(n_src, trace_values, trace_owner, trace_source, source_fields, green_fields):
    values = trace_values[0]
    sources_here = source_fields.shape[1]
    slab = lax.axis_index("slab")
    src = lax.axis_index("src")
    x, c = slab // 2, slab % 2
    z, y = src // 2, src % 2
    lines = range(n_src // 2)

    def send(array, moves):
        pairs = [
            (number(*a, n_src), number(*b, n_src)) for a, b in moves
        ]
        return lax.ppermute(array, AXES, pairs)

    everywhere = [
        (a, b, d, e) for a in range(2) for b in range(2) for d in range(2) for e in lines
    ]
    to_core = [((a, b, d, e), (a, 1 - b, d, e)) for a, b, d, e in everywhere]
    to_x = [((a, b, d, e), (1 - a, b, d, e)) for a, b, d, e in everywhere]
    to_both = [((a, b, d, e), (1 - a, 1 - b, d, e)) for a, b, d, e in everywhere]

    def after(array, *earlier):
        return lax.optimization_barrier((array, *earlier))[0]

    place_x = jnp.stack([x]).astype(jnp.int32)
    ids = id_rows(trace_owner, trace_source, sources_here)
    kept, away = cut(place_x, values, ids)
    kept_core = send(kept, to_core)
    own = join(kept, kept_core)
    crossed_here = after(send(away, to_x), own)
    crossed = join(crossed_here, send(crossed_here, to_core))

    moves = []
    for steps in (
        [(0, 0, 1, None), (1, 0, 1, 1), (0, 1, 0, 0), (1, 1, 0, 2)],
        [(0, 0, 1, None), (1, 0, 0, 1), (0, 1, 0, 0), (1, 1, 1, 2)],
        [(0, 0, 1, None), (1, 0, 1, 1), (0, 1, 0, 2), (1, 1, 0, 0)],
        [(0, 0, 1, None), (1, 1, 1, 2)],
        [(1, 0, 1, 1), (0, 1, 1, 0)],
    ):
        pairs = []
        for here_c, here_z, there_c, there_z in steps:
            for a in range(2):
                for d in range(2):
                    for e in (here_z, len(lines) - 1 - here_z):
                        if there_z is None:
                            target = (a, there_c, 1 - d, e)
                        else:
                            far_z = there_z if e == here_z else len(lines) - 1 - there_z
                            target = (a, there_c, d, far_z)
                        pairs.append(((a, here_c, d, e), target))
        moves.append(pairs)
    brought = np.array(
        [
            [[(1, 0), (2, 0), (3, 0), (0, 0)], [(0, 1), (1, 1), (2, 1), (3, 1)]],
            [[(2, 0), (0, 1), (3, 1), (1, 0)], [(0, 0), (3, 0), (1, 1), (2, 1)]],
        ],
        np.int32,
    )
    mirrored = brought[::-1].copy()
    mirrored[..., 0] = len(lines) - 1 - mirrored[..., 0]
    table = jnp.asarray(np.concatenate([brought, mirrored]))

    mine_now = lax.dynamic_index_in_dim(
        lax.dynamic_index_in_dim(table, z, 0, keepdims=False), c, 0, keepdims=False
    )
    groups = jnp.bitwise_xor(mine_now[:, 0], slab)
    on_line = jnp.bitwise_xor(mine_now[:, 1], y)
    where_green = jnp.stack([groups, on_line], axis=1).reshape(-1)
    place = jnp.concatenate(
        [jnp.stack([slab]), where_green, jnp.stack([1 - c])]
    ).astype(jnp.int32)
    sources = 4 * sources_here

    blocks = green_fields.reshape(2, 2, 2, -1, green_fields.shape[2])
    made = {"own": own, "crossed": crossed, "crossed_here": crossed_here}
    steps = {}

    def get(name):
        if name not in made:
            made[name] = None
            made[name] = steps[name]()
        return made[name]

    def behind(name, array):
        return after(array, *[get(k) for k in ORDER.get(name, ())])

    steps["r1_a"] = lambda: send(own, moves[0])
    steps["r2_a"] = lambda: send(behind("r2_a", get("r1_a")), moves[1])
    steps["r3_a"] = lambda: send(behind("r3_a", get("r2_a")), moves[2])
    steps["r4_a"] = lambda: send(behind("r4_a", get("r3_a")), moves[3])
    steps["r1_b"] = lambda: send(behind("r1_b", crossed), moves[0])
    steps["r2_b"] = lambda: send(behind("r2_b", get("r1_b")), moves[1])
    steps["r3_b"] = lambda: send(behind("r3_b", get("r2_b")), moves[2])
    steps["r4_b"] = lambda: send(behind("r4_b", get("r3_b")), moves[4])
    steps["res_1"] = lambda: residual(
        place, (get("r1_a"), behind("res_1", get("r1_b"))), sources
    )
    steps["res_2"] = lambda: residual(
        place, (get("r2_a"), behind("res_2", get("r2_b"))), sources
    )
    steps["res_3"] = lambda: residual(
        place, (get("r3_a"), behind("res_3", get("r3_b"))), sources
    )
    steps["begun"] = lambda: begin(place, (behind("begun", get("r4_a")), own), sources)
    steps["field_core"] = lambda: send(behind("field_core", source_fields), to_core)
    steps["field_x"] = lambda: send(behind("field_x", source_fields), to_x)
    steps["field_far"] = lambda: send(behind("field_far", get("field_x")), to_core)
    steps["halves"] = lambda: halves(place_x, behind("halves", blocks))
    steps["near"] = lambda: get("halves")[0]
    steps["away"] = lambda: get("halves")[1]
    steps["near_core"] = lambda: send(behind("near_core", get("near")), to_core)
    steps["far"] = lambda: send(behind("far", get("away")), to_x)
    steps["far_core"] = lambda: send(behind("far_core", get("far")), to_core)
    steps["fields"] = lambda: (
        source_fields, get("field_core"), get("field_x"), get("field_far")
    )
    steps["early"] = lambda: correlated(
        (get("res_1"), behind("early", get("res_2"))), get("fields")
    )
    steps["middle"] = lambda: correlated(
        (behind("middle", get("res_3")),), get("fields")
    )
    greens = [get(k) for k in ("near", "near_core", "far", "far_core")]
    folded = fold(
        place, (get("early"), behind("fold", get("middle"))), greens
    )
    partial = last(
        place, (get("r4_b"), crossed), get("begun"), folded, greens, get("fields")
    )[0]
    here = partial + send(partial, to_core)
    there = send(partial, to_x) + send(partial, to_both)
    return here + there


def gathered(trace_values, trace_owner, trace_source, source_fields, green_fields):
    values = trace_values[0]
    half_width = values.shape[1] // 2
    src_count = lax.axis_size("src")
    sources_here = source_fields.shape[1]
    slab_index = lax.axis_index("slab")
    high = trace_owner[0, :, 0] * (sources_here // 32) + trace_source[0] // 32
    low = trace_source[0] % 32
    per_slab = sources_here // 32
    piece_values = lax.all_gather(values, "slab", axis=0, tiled=True)
    owners = trace_owner[0, :, 0].astype(jnp.bfloat16)
    high_part = (trace_source[0] // 32).astype(jnp.bfloat16)
    low_part = low.astype(jnp.bfloat16)
    piece_ids = lax.all_gather(
        jnp.stack([owners, high_part, low_part]), "slab", axis=1, tiled=True
    )
    ids = jnp.arange(sources_here, dtype=jnp.int32)
    picks = (
        ((ids // 32).astype(jnp.bfloat16)[:, None] == piece_ids[1][None, :])
        & ((ids % 32).astype(jnp.bfloat16)[:, None] == piece_ids[2][None, :])
        & (piece_ids[0][None, :] == slab_index.astype(jnp.bfloat16))
    )
    assembled = jnp.dot(
        picks.astype(jnp.bfloat16), piece_values, preferred_element_type=jnp.float32
    )
    rows = lax.all_gather(assembled.astype(jnp.bfloat16), "src", axis=1, tiled=True)
    split_rows = rows.reshape(sources_here, src_count, 2, half_width)
    res_real = split_rows[:, :, 0, :].reshape(sources_here, src_count * half_width)
    res_imag = split_rows[:, :, 1, :].reshape(sources_here, src_count * half_width)
    green = lax.all_gather(green_fields, "slab", axis=1, tiled=True)
    dot = functools.partial(jnp.dot, preferred_element_type=jnp.float32)
    adj_real = dot(res_real, green[0]) + dot(res_imag, green[1])
    adj_imag = dot(res_real, green[1]) - dot(res_imag, green[0])
    partial = jnp.sum(
        source_fields[0].astype(jnp.float32) * adj_real
        - source_fields[1].astype(jnp.float32) * adj_imag,
        axis=0,
    )
    return lax.psum(partial, "slab")


def solution(mesh):
    in_specs = (
        P("src", "slab", None),
        P("src", "slab", None),
        P("src", "slab"),
        P(None, "slab", "src"),
        P(None, "slab", "src"),
    )
    n_slab, n_src = mesh.shape["slab"], mesh.shape["src"]
    if n_slab == 2 * 2 and n_src == 2 * 4:
        on_device = functools.partial(paired, n_src)
    else:
        on_device = gathered
    return jax.shard_map(
        on_device, mesh=mesh, in_specs=in_specs, out_specs=P("src"), check_vma=False
    )
```

```python
import functools

import jax
import jax.numpy as jnp
import numpy as np
from jax import lax
from jax.experimental import pallas as pl
from jax.experimental.pallas import tpu as pltpu
from jax.sharding import PartitionSpec as P

AXES = ("slab", "src")
PAD = 16
TILE = 256
VMEM_LIMIT = 24 * 1024 * 1024


def params():
    return pltpu.CompilerParams(vmem_limit_bytes=VMEM_LIMIT)


def light():
    return pl.CostEstimate(flops=1000, bytes_accessed=1000, transcendentals=0)


SMEM_SPEC = pl.BlockSpec(memory_space=pltpu.SMEM)
VMEM_SPEC = pl.BlockSpec(memory_space=pltpu.VMEM)


ORDER = {
    "r4_a": ("res_1",),
    "r4_b": ("res_2",),
    "res_1": ("r2_a",),
    "res_2": ("r3_a",),
    "field_core": ("r1_a",),
    "field_x": ("own",),
    "field_far": ("res_1",),
    "halves": ("r1_a",),
    "far": ("r3_a", "near_core",),
    "res_3": ("early",),
    "far_core": ("res_3",),
    "near_core": ("r2_a",),
}


def number(x, c, y, z, n_src):
    return (2 * x + c) * n_src + 2 * z + y


def receivers(values, first, rows, out_ref, spot):
    quarter = values.shape[1] // 4
    for part in range(2):
        low = values[:, 2 * part * quarter : (2 * part + 1) * quarter]
        high = values[:, (2 * part + 1) * quarter : (2 * part + 2) * quarter]
        lanes = pl.ds(part * quarter, quarter)
        out_ref[pl.ds(spot, rows), lanes] = jnp.where(first, low, high)


def id_rows(trace_owner, trace_source, sources_here):
    ids = trace_source[0]
    high = trace_owner[0, :, 0] * (sources_here // TILE) + ids // TILE
    rows = jnp.stack([high, ids % TILE])
    return jnp.pad(rows, ((0, PAD - 2), (0, 0))).astype(jnp.bfloat16)


def cut_kernel(place, values, ids, near_ref, away_ref):
    rows = values.shape[0]
    first = place[0] == 0
    receivers(values, first, rows, near_ref, 0)
    receivers(values, jnp.logical_not(first), rows, away_ref, 0)
    tiles = rows // TILE
    block = jnp.concatenate(
        [
            ids[kind : kind + 1, j * TILE : (j + 1) * TILE]
            for kind in range(2)
            for j in range(tiles)
        ]
        + [jnp.zeros((PAD - 2 * tiles, TILE), jnp.bfloat16)],
        axis=0,
    )
    near_ref[rows:, :] = block
    away_ref[rows:, :] = block


def cut(place, values, ids):
    rows, width = values.shape
    shape = jax.ShapeDtypeStruct((rows + PAD, width // 2), jnp.bfloat16)
    return pl.pallas_call(
        cut_kernel,
        name="cut",
        out_shape=(shape, shape),
        in_specs=[SMEM_SPEC] + [VMEM_SPEC] * 2,
        out_specs=(VMEM_SPEC, VMEM_SPEC),
        compiler_params=params(),
        cost_estimate=light(),
    )(place, values, ids)


def join_kernel(mine, other, out_ref):
    rows = mine.shape[0] - PAD
    tiles = rows // TILE
    out_ref[:rows, :] = mine[:rows, :]
    out_ref[rows : 2 * rows, :] = other[:rows, :]
    ids = [mine[rows:, :], other[rows:, :]]
    pieces = [part[kind * tiles : (kind + 1) * tiles] for kind in range(2) for part in ids]
    pad = jnp.zeros((PAD - 4 * tiles, TILE), jnp.bfloat16)
    out_ref[2 * rows :, :] = jnp.concatenate(pieces + [pad], axis=0)


def join(mine, other):
    rows, width = mine.shape
    return pl.pallas_call(
        join_kernel,
        name="join",
        out_shape=jax.ShapeDtypeStruct((2 * rows - PAD, width), jnp.bfloat16),
        in_specs=[VMEM_SPEC] * 2,
        out_specs=VMEM_SPEC,
        compiler_params=params(),
        cost_estimate=light(),
    )(mine, other)


def halves_kernel(place, blocks, near_ref, away_ref):
    first = place[0] == 0
    for p in range(blocks.shape[0]):
        for line in range(blocks.shape[1]):
            low, high = blocks[p, line, 0], blocks[p, line, 1]
            near_ref[p, line] = jnp.where(first, low, high)
            away_ref[p, line] = jnp.where(first, high, low)


def halves(place, blocks):
    shape = jax.ShapeDtypeStruct(blocks.shape[:2] + blocks.shape[3:], blocks.dtype)
    return pl.pallas_call(
        halves_kernel,
        name="halves",
        out_shape=(shape, shape),
        in_specs=[SMEM_SPEC, VMEM_SPEC],
        out_specs=(VMEM_SPEC, VMEM_SPEC),
        compiler_params=params(),
        cost_estimate=light(),
    )(place, blocks)


def choose(which, candidates, target):
    first, second = candidates
    target[...] = jnp.where(which == 0, first[...], second[...])


def assemble(slab, pieces, group, per, start=None):
    traces = pieces[0].shape[0] - PAD
    tiles = traces // TILE
    iota = lax.broadcasted_iota(jnp.int32, (TILE, TILE), 0).astype(jnp.bfloat16)
    out = []
    owner = slab ^ group
    for h in range(per):
        name = (owner * per + h).astype(jnp.float32).astype(jnp.bfloat16)
        total = None if start is None else start[h * TILE : (h + 1) * TILE, :]
        for piece in pieces:
            masks = []
            for j in range(tiles):
                high = piece[traces + j : traces + j + 1, :]
                low = piece[traces + tiles + j : traces + tiles + j + 1, :]
                wanted = jnp.where(high == name, low, jnp.bfloat16(-1.0))
                masks.append(
                    jnp.where(iota == wanted, jnp.bfloat16(1.0), jnp.bfloat16(0.0))
                )
            mask = jnp.concatenate(masks, axis=1)
            term = jnp.dot(
                mask, piece[:traces, :], preferred_element_type=jnp.float32
            )
            total = term if total is None else total + term
        out.append(total)
    return jnp.concatenate(out, axis=0)


def residual_kernel(n, place, *refs):
    out_ref = refs[n]
    rows = out_ref.shape[0] // 4
    for group in range(4):
        out_ref[group * rows : (group + 1) * rows, :] = assemble(
            place[0], refs[:n], group, rows // TILE
        ).astype(out_ref.dtype)


def residual(place, pieces, sources):
    return pl.pallas_call(
        functools.partial(residual_kernel, len(pieces)),
        name="residual",
        out_shape=jax.ShapeDtypeStruct((sources, pieces[0].shape[1]), jnp.bfloat16),
        in_specs=[SMEM_SPEC] + [VMEM_SPEC] * len(pieces),
        out_specs=VMEM_SPEC,
        compiler_params=params(),
        cost_estimate=light(),
    )(place, *pieces)


def begin_kernel(n, place, *refs):
    cand, (out_ref, piece) = refs[:n], refs[n:]
    choose(place[9], cand, piece)
    rows = out_ref.shape[0] // 4
    for group in range(4):
        out_ref[group * rows : (group + 1) * rows, :] = assemble(
            place[0], (piece,), group, rows // TILE
        )


def begin(place, cand, sources):
    shape = cand[0].shape
    return pl.pallas_call(
        functools.partial(begin_kernel, len(cand)),
        name="begin",
        out_shape=jax.ShapeDtypeStruct((sources, shape[1]), jnp.float32),
        in_specs=[SMEM_SPEC] + [VMEM_SPEC] * len(cand),
        out_specs=VMEM_SPEC,
        scratch_shapes=[pltpu.VMEM(shape, jnp.bfloat16)],
        compiler_params=params(),
        cost_estimate=light(),
    )(place, *cand)


def correlate(res, fields):
    contract = (((0,), (0,)), ((), ()))
    dot = functools.partial(
        lax.dot_general,
        dimension_numbers=contract,
        preferred_element_type=jnp.float32,
    )
    half = res[0].shape[1] // 2
    real, imag = None, None
    for piece, field in zip(res, fields):
        with_real, with_imag = dot(piece, field[0]), dot(piece, field[1])
        first = with_real[:half] + with_imag[half:]
        second = with_real[half:] - with_imag[:half]
        real = first if real is None else real + first
        imag = second if imag is None else imag + second
    return real, imag


def correlate_kernel(n_res, *refs):
    res, out_ref = refs[:n_res], refs[-1]
    fields = refs[n_res:-1]
    rows = res[0].shape[0] // 4
    for k, ref in enumerate(res):
        parts = [ref[g * rows : (g + 1) * rows, :] for g in range(4)]
        real, imag = correlate(parts, fields)
        out_ref[k, 0] = real
        out_ref[k, 1] = imag


def correlated(res, fields):
    half, cells = res[0].shape[1] // 2, fields[0].shape[2]
    return pl.pallas_call(
        functools.partial(correlate_kernel, len(res)),
        name="correlate",
        out_shape=jax.ShapeDtypeStruct((len(res), 2, half, cells), jnp.float32),
        in_specs=[VMEM_SPEC] * (len(res) + len(fields)),
        out_specs=VMEM_SPEC,
        compiler_params=params(),
        cost_estimate=light(),
    )(*res, *fields)


def fetch_green(place, slot, greens, target, sems):
    group, line = place[1 + 2 * slot], place[2 + 2 * slot]
    for j, ref in enumerate(greens):

        @pl.when(group == j)
        def _(ref=ref):
            for p in range(2):
                pltpu.make_async_copy(ref.at[p, line], target.at[p], sems.at[p]).start()

    def wait():
        for p in range(2):
            pltpu.make_async_copy(greens[0].at[p, 0], target.at[p], sems.at[p]).wait()

    return wait


def fold_kernel(n, place, *refs):
    factors, greens, (out_ref, green, sems) = refs[:n], refs[n : n + 4], refs[n + 4 :]
    slots = [(ref, k) for ref in factors for k in range(ref.shape[0])]
    waits = [
        fetch_green(place, j, greens, green.at[j], sems.at[j])
        for j in range(len(slots))
    ]
    total = None
    for j, (ref, k) in enumerate(slots):
        waits[j]()
        for p in range(2):
            term = green[j, p].astype(jnp.float32) * ref[k, p]
            total = term if total is None else total + term
    out_ref[...] = jnp.sum(total, axis=0, keepdims=True)


def fold(place, factors, greens):
    slots = sum(f.shape[0] for f in factors)
    return pl.pallas_call(
        functools.partial(fold_kernel, len(factors)),
        name="fold",
        out_shape=jax.ShapeDtypeStruct((1, factors[0].shape[3]), jnp.float32),
        in_specs=[SMEM_SPEC] + [VMEM_SPEC] * (len(factors) + len(greens)),
        out_specs=VMEM_SPEC,
        scratch_shapes=[
            pltpu.VMEM((slots, 2) + greens[0].shape[2:], jnp.bfloat16),
            pltpu.SemaphoreType.DMA((slots, 2)),
        ],
        compiler_params=params(),
        cost_estimate=light(),
    )(place, *factors, *greens)


def last_kernel(n_b, place, *refs):
    cand_b, (begun, folded) = refs[:n_b], refs[n_b : n_b + 2]
    greens, fields = refs[n_b + 2 : n_b + 6], refs[n_b + 6 : n_b + 10]
    out_ref, piece, green, sems = refs[n_b + 10 :]
    wait = fetch_green(place, 3, greens, green, sems)
    choose(place[9], cand_b, piece)
    rows = begun.shape[0] // 4
    parts = [
        assemble(
            place[0],
            (piece,),
            g,
            rows // TILE,
            begun[g * rows : (g + 1) * rows, :],
        ).astype(jnp.bfloat16)
        for g in range(4)
    ]
    real, imag = correlate(parts, fields)
    wait()
    total = green[0].astype(jnp.float32) * real + green[1].astype(jnp.float32) * imag
    out_ref[...] = folded[...] + jnp.sum(total, axis=0, keepdims=True)


def last(place, cand_b, begun, folded, greens, fields):
    return pl.pallas_call(
        functools.partial(last_kernel, len(cand_b)),
        name="last",
        out_shape=jax.ShapeDtypeStruct(folded.shape, jnp.float32),
        in_specs=[SMEM_SPEC]
        + [VMEM_SPEC] * (len(cand_b) + 2 + len(greens) + len(fields)),
        out_specs=VMEM_SPEC,
        scratch_shapes=[
            pltpu.VMEM(cand_b[0].shape, jnp.bfloat16),
            pltpu.VMEM((2,) + greens[0].shape[2:], jnp.bfloat16),
            pltpu.SemaphoreType.DMA((2,)),
        ],
        compiler_params=params(),
        cost_estimate=light(),
    )(place, *cand_b, begun, folded, *greens, *fields)


def paired(n_src, trace_values, trace_owner, trace_source, source_fields, green_fields):
    values = trace_values[0]
    sources_here = source_fields.shape[1]
    slab = lax.axis_index("slab")
    src = lax.axis_index("src")
    x, c = slab // 2, slab % 2
    z, y = src // 2, src % 2
    lines = range(n_src // 2)

    def send(array, moves):
        pairs = [
            (number(*a, n_src), number(*b, n_src)) for a, b in moves
        ]
        return lax.ppermute(array, AXES, pairs)

    everywhere = [
        (a, b, d, e) for a in range(2) for b in range(2) for d in range(2) for e in lines
    ]
    to_core = [((a, b, d, e), (a, 1 - b, d, e)) for a, b, d, e in everywhere]
    to_x = [((a, b, d, e), (1 - a, b, d, e)) for a, b, d, e in everywhere]

    def after(array, *earlier):
        return lax.optimization_barrier((array, *earlier))[0]

    place_x = jnp.stack([x]).astype(jnp.int32)
    ids = id_rows(trace_owner, trace_source, sources_here)
    kept, away = cut(place_x, values, ids)
    kept_core = send(kept, to_core)
    own = join(kept, kept_core)
    crossed_here = after(send(away, to_x), own)
    crossed = join(crossed_here, send(crossed_here, to_core))

    moves = []
    for steps in (
        [(0, 0, 1, None), (1, 0, 1, 1), (0, 1, 0, 0), (1, 1, 0, 2)],
        [(0, 0, 1, None), (1, 0, 0, 1), (0, 1, 0, 0), (1, 1, 1, 2)],
        [(0, 0, 1, None), (1, 0, 1, 1), (0, 1, 0, 2), (1, 1, 0, 0)],
        [(0, 0, 1, None), (1, 1, 1, 2)],
        [(1, 0, 1, 1), (0, 1, 1, 0)],
    ):
        pairs = []
        for here_c, here_z, there_c, there_z in steps:
            for a in range(2):
                for d in range(2):
                    for e in (here_z, len(lines) - 1 - here_z):
                        if there_z is None:
                            target = (a, there_c, 1 - d, e)
                        else:
                            far_z = there_z if e == here_z else len(lines) - 1 - there_z
                            target = (a, there_c, d, far_z)
                        pairs.append(((a, here_c, d, e), target))
        moves.append(pairs)
    brought = np.array(
        [
            [[(1, 0), (2, 0), (3, 0), (0, 0)], [(0, 1), (1, 1), (2, 1), (3, 1)]],
            [[(2, 0), (0, 1), (3, 1), (1, 0)], [(0, 0), (3, 0), (1, 1), (2, 1)]],
        ],
        np.int32,
    )
    mirrored = brought[::-1].copy()
    mirrored[..., 0] = len(lines) - 1 - mirrored[..., 0]
    table = jnp.asarray(np.concatenate([brought, mirrored]))

    mine_now = lax.dynamic_index_in_dim(
        lax.dynamic_index_in_dim(table, z, 0, keepdims=False), c, 0, keepdims=False
    )
    groups = jnp.bitwise_xor(mine_now[:, 0], slab)
    on_line = jnp.bitwise_xor(mine_now[:, 1], y)
    where_green = jnp.stack([groups, on_line], axis=1).reshape(-1)
    place = jnp.concatenate(
        [jnp.stack([slab]), where_green, jnp.stack([1 - c])]
    ).astype(jnp.int32)
    sources = 4 * sources_here

    blocks = green_fields.reshape(2, 2, 2, -1, green_fields.shape[2])
    made = {"own": own, "crossed": crossed, "crossed_here": crossed_here}
    steps = {}

    def get(name):
        if name not in made:
            made[name] = None
            made[name] = steps[name]()
        return made[name]

    def behind(name, array):
        return after(array, *[get(k) for k in ORDER.get(name, ())])

    steps["r1_a"] = lambda: send(own, moves[0])
    steps["r2_a"] = lambda: send(behind("r2_a", get("r1_a")), moves[1])
    steps["r3_a"] = lambda: send(behind("r3_a", get("r2_a")), moves[2])
    steps["r4_a"] = lambda: send(behind("r4_a", get("r3_a")), moves[3])
    steps["r1_b"] = lambda: send(behind("r1_b", crossed), moves[0])
    steps["r2_b"] = lambda: send(behind("r2_b", get("r1_b")), moves[1])
    steps["r3_b"] = lambda: send(behind("r3_b", get("r2_b")), moves[2])
    steps["r4_b"] = lambda: send(behind("r4_b", get("r3_b")), moves[4])
    steps["res_1"] = lambda: residual(
        place, (get("r1_a"), behind("res_1", get("r1_b"))), sources
    )
    steps["res_2"] = lambda: residual(
        place, (get("r2_a"), behind("res_2", get("r2_b"))), sources
    )
    steps["res_3"] = lambda: residual(
        place, (get("r3_a"), behind("res_3", get("r3_b"))), sources
    )
    steps["begun"] = lambda: begin(place, (behind("begun", get("r4_a")), own), sources)
    steps["field_core"] = lambda: send(behind("field_core", source_fields), to_core)
    steps["field_x"] = lambda: send(behind("field_x", source_fields), to_x)
    steps["field_far"] = lambda: send(behind("field_far", get("field_x")), to_core)
    steps["halves"] = lambda: halves(place_x, behind("halves", blocks))
    steps["near"] = lambda: get("halves")[0]
    steps["away"] = lambda: get("halves")[1]
    steps["near_core"] = lambda: send(behind("near_core", get("near")), to_core)
    steps["far"] = lambda: send(behind("far", get("away")), to_x)
    steps["far_core"] = lambda: send(behind("far_core", get("far")), to_core)
    steps["fields"] = lambda: (
        source_fields, get("field_core"), get("field_x"), get("field_far")
    )
    steps["early"] = lambda: correlated(
        (get("res_1"), behind("early", get("res_2"))), get("fields")
    )
    steps["middle"] = lambda: correlated(
        (behind("middle", get("res_3")),), get("fields")
    )
    greens = [get(k) for k in ("near", "near_core", "far", "far_core")]
    folded = fold(
        place, (get("early"), behind("fold", get("middle"))), greens
    )
    partial = last(
        place, (get("r4_b"), crossed), get("begun"), folded, greens, get("fields")
    )[0]
    chip = partial + send(partial, to_core)
    return chip + send(chip, to_x)


def gathered(trace_values, trace_owner, trace_source, source_fields, green_fields):
    values = trace_values[0]
    half_width = values.shape[1] // 2
    src_count = lax.axis_size("src")
    sources_here = source_fields.shape[1]
    slab_index = lax.axis_index("slab")
    high = trace_owner[0, :, 0] * (sources_here // 32) + trace_source[0] // 32
    low = trace_source[0] % 32
    per_slab = sources_here // 32
    piece_values = lax.all_gather(values, "slab", axis=0, tiled=True)
    owners = trace_owner[0, :, 0].astype(jnp.bfloat16)
    high_part = (trace_source[0] // 32).astype(jnp.bfloat16)
    low_part = low.astype(jnp.bfloat16)
    piece_ids = lax.all_gather(
        jnp.stack([owners, high_part, low_part]), "slab", axis=1, tiled=True
    )
    ids = jnp.arange(sources_here, dtype=jnp.int32)
    picks = (
        ((ids // 32).astype(jnp.bfloat16)[:, None] == piece_ids[1][None, :])
        & ((ids % 32).astype(jnp.bfloat16)[:, None] == piece_ids[2][None, :])
        & (piece_ids[0][None, :] == slab_index.astype(jnp.bfloat16))
    )
    assembled = jnp.dot(
        picks.astype(jnp.bfloat16), piece_values, preferred_element_type=jnp.float32
    )
    rows = lax.all_gather(assembled.astype(jnp.bfloat16), "src", axis=1, tiled=True)
    split_rows = rows.reshape(sources_here, src_count, 2, half_width)
    res_real = split_rows[:, :, 0, :].reshape(sources_here, src_count * half_width)
    res_imag = split_rows[:, :, 1, :].reshape(sources_here, src_count * half_width)
    green = lax.all_gather(green_fields, "slab", axis=1, tiled=True)
    dot = functools.partial(jnp.dot, preferred_element_type=jnp.float32)
    adj_real = dot(res_real, green[0]) + dot(res_imag, green[1])
    adj_imag = dot(res_real, green[1]) - dot(res_imag, green[0])
    partial = jnp.sum(
        source_fields[0].astype(jnp.float32) * adj_real
        - source_fields[1].astype(jnp.float32) * adj_imag,
        axis=0,
    )
    return lax.psum(partial, "slab")


def solution(mesh):
    in_specs = (
        P("src", "slab", None),
        P("src", "slab", None),
        P("src", "slab"),
        P(None, "slab", "src"),
        P(None, "slab", "src"),
    )
    n_slab, n_src = mesh.shape["slab"], mesh.shape["src"]
    if n_slab == 2 * 2 and n_src == 2 * 4:
        on_device = functools.partial(paired, n_src)
    else:
        on_device = gathered
    return jax.shard_map(
        on_device, mesh=mesh, in_specs=in_specs, out_specs=P("src"), check_vma=False
    )
```
